512 devices in a mesh: row: 16 (over y, x_lo, core), col: 32 (over z, x_hi).
Axes of the slice: x: 4 (x_hi: 2, x_lo: 2; x = x_hi * 2 + x_lo), y: 4, z: 16, core: 2. Of those that a mesh axis runs over, the one named last changes fastest.
Arguments:
- object_field: float32 [2, 4096, 8192], P(None, 'row', 'col'), may hold values from -6 to 6
- probe: float32 [2, 256, 256], replicated, may hold values from -6 to 6
- counts_measured: float32 [16, 32, 4, 256, 256], P('row', 'col'), may hold values from 0.05 to 6
- offsets: int32 [16, 32, 4, 2], P('row', 'col'), may hold values from 0 to 255
- slot_count: int32 [16, 32], P('row', 'col'), may hold values from 1 to 4, as said below
Outputs:
- object_grad: float32 [2, 4096, 8192], P(None, 'row', 'col')
- probe_step: float32 [2, 256, 256], replicated
The draws below stay inside these ranges and needn't reach their ends.
Inputs may be any that keep to these rules, and one draw needn't show every extreme that they name: `slot_count`: of the two tiles (a, b) and (a, b + 16) one lists more than 2 positions and the other fewer than 2; some tile lists 4. Offsets lie inside the tile; slots at or beyond a tile's count hold offsets too but are not used.
All inputs are finite; a program needn't handle non-finite values.
Results may differ from the reference program's by a relative error of at most 0.0003.
Values sent between devices are 32-bit elements; how exact they have to be, the bound alone decides.
A program may use at most 192 MiB of HBM per device.

```python
import math
import jax
import jax.numpy as jnp
from jax import lax

PS = 256
TILE = 256
CAP = 4
HALF = 2
TILE_ROWS = 16
TILE_COLS = 32
NY = 4096
NX = 8192


def draw_slot_count(key, part):
    key = jax.random.fold_in(key, 11)
    first, second, third, fourth = jax.random.split(key, 4)
    pairs = TILE_ROWS * (TILE_COLS // 2)
    heavy = jax.random.randint(first, (pairs,), HALF + 1, CAP + 1)
    chosen = jax.random.randint(second, (), 0, pairs)
    heavy = jnp.where(jnp.arange(pairs) == chosen, CAP, heavy)
    light = jax.random.randint(third, (pairs,), 1, HALF)
    flip = jax.random.randint(fourth, (pairs,), 0, 2)
    left = jnp.where(flip == 1, heavy, light).reshape(TILE_ROWS, TILE_COLS // 2)
    right = jnp.where(flip == 1, light, heavy).reshape(TILE_ROWS, TILE_COLS // 2)
    return jnp.concatenate([left, right], axis=1).astype(jnp.int32)


def set_ends(array, rng, least, largest):
    dims = array.shape
    spot = [jax.random.randint(jax.random.fold_in(rng, axis), (), 0, dims[axis]) for axis in range(len(dims))]
    array = array.at[tuple(spot)].set(least)
    longest = dims.index(max(dims))
    spot[longest] = (spot[longest] + 1) % dims[longest]
    return array.at[tuple(spot)].set(largest)


def level_of(key, dims, shards, least, largest):
    def one(position, parts):
        heights = jax.random.uniform(jax.random.fold_in(jax.random.fold_in(key, 6), position), (parts,), jnp.float32, least / len(shards), largest / len(shards))
        return jnp.repeat(jnp.exp(heights), dims[position] // parts).reshape((-1,) + (1,) * (len(dims) - position - 1))

    factor_of = one(*shards[0])
    for cut in shards[1:]:
        factor_of = factor_of * one(*cut)
    return factor_of


def noise(rng, shape, deviation, limit, cuts=(), held_as=jnp.bfloat16):
    factor_of = level_of(rng, shape, cuts, -0.22, 0.18) if cuts else 1.0
    entries = jax.random.normal(rng, shape, jnp.float32) * deviation * factor_of
    return jnp.minimum(jnp.maximum(entries, -limit), limit).astype(held_as)


def setup_inputs(seed: int = 0) -> dict:
    splits = jax.random.split(jax.random.key(seed), 6)
    return {
        "object_field": noise(splits[0], (2, NY, NX), 1.0, 6.0, ((1, 16), (2, 32)), jnp.float32),
        "probe": noise(splits[1], (2, PS, PS), 1.0, 6.0, (), jnp.float32),
        "counts_measured": jnp.clip(jnp.exp(math.log(6.0) - 4.787492 * jax.random.uniform(splits[2], (TILE_ROWS, TILE_COLS, CAP, PS, PS), jnp.float32) ** level_of(splits[2], (TILE_ROWS, TILE_COLS, CAP, PS, PS), ((0, 16), (1, 32)), -0.2, 0.2)), 0.05, 6.0),
        "offsets": set_ends(jax.random.randint(splits[3], (TILE_ROWS, TILE_COLS, CAP, 2), 0, TILE), jax.random.fold_in(splits[3], 1), 0, TILE - 1).astype(jnp.int32),
        "slot_count": draw_slot_count(jax.random.fold_in(splits[5], 71), 0),
    }


def reference(object_field, probe, counts_measured, offsets, slot_count):
    padded = jnp.pad(object_field, ((0, 0), (0, PS), (0, PS)))
    probe_c = probe[0] + 1j * probe[1]
    total = TILE_ROWS * TILE_COLS * CAP
    flat_counts = counts_measured.reshape(total, PS, PS)
    flat_offsets = offsets.reshape(total, 2)
    indices = jnp.arange(total, dtype=jnp.int32)

    def step(carry, item):
        grad, gprobe, illum = carry
        index, measured, offs = item
        tile_row = index // (TILE_COLS * CAP)
        tile_col = index // CAP % TILE_COLS
        slot = index % CAP
        valid = (slot < slot_count[tile_row, tile_col]).astype(jnp.float32)
        start_y = (tile_row * TILE + offs[0]).astype(jnp.int32)
        start_x = (tile_col * TILE + offs[1]).astype(jnp.int32)
        zero = jnp.int32(0)
        patch = lax.dynamic_slice(padded, (zero, start_y, start_x), (2, PS, PS))
        patch_c = patch[0] + 1j * patch[1]
        wave = jnp.fft.fft2(probe_c * patch_c, norm='ortho')
        model = jnp.real(wave) ** 2 + jnp.imag(wave) ** 2 + 0.5
        chi = jnp.fft.ifft2((1.0 - measured / model) * wave, norm='ortho')
        gpatch = jnp.conj(probe_c) * chi
        gpatch = jnp.stack([jnp.real(gpatch), jnp.imag(gpatch)]) * valid
        current = lax.dynamic_slice(grad, (zero, start_y, start_x), (2, PS, PS))
        grad = lax.dynamic_update_slice(grad, current + gpatch, (zero, start_y, start_x))
        gterm = jnp.conj(patch_c) * chi
        gprobe = gprobe + jnp.stack([jnp.real(gterm), jnp.imag(gterm)]) * valid
        illum = illum + (patch[0] * patch[0] + patch[1] * patch[1]) * valid
        return ((grad, gprobe, illum), None)
    init = (jnp.zeros_like(padded), jnp.zeros((2, PS, PS), jnp.float32), jnp.zeros((PS, PS), jnp.float32))
    (grad, gprobe, illum), unused = lax.scan(step, init, (indices, flat_counts, flat_offsets))
    object_grad = grad[:, :NY, :NX]
    probe_step = gprobe / jnp.sqrt(illum + 1.0)
    return (object_grad, probe_step)
```

```python
import functools
import math

import jax
import jax.numpy as jnp
import ml_dtypes
import numpy as np
from jax import lax
from jax.experimental import pallas as pl
from jax.experimental.pallas import tpu as pltpu
from jax.sharding import PartitionSpec as P

MESH = pl.DeviceIdType.MESH
PS = 256
HALF = 128
CAP = 4
CHUNKS = 4
ROWS = PS // CHUNKS
PLANE = 16
OWNERS = 4
F32 = jnp.float32
BF16 = jnp.bfloat16


def split_bf16(table):
    high = table.astype(ml_dtypes.bfloat16)
    low = (table - high.astype(np.float64)).astype(ml_dtypes.bfloat16)
    return high, low


def constants():
    n = np.arange(HALF)
    angle = 2.0 * math.pi * ((n[:, None] * n[None, :]) % HALF) / HALF
    cos, sin = np.cos(angle) / 16.0, np.sin(angle) / 16.0
    matrix = np.block([[cos, -sin], [sin, cos]])
    high, low = split_bf16(matrix)
    high_t, low_t = split_bf16(matrix.T)
    tables = np.stack([high, low, high_t, low_t])
    turn = 2.0 * math.pi * n / PS
    tw = np.stack([np.cos(turn), -np.sin(turn)]).astype(np.float32)
    lane_tw = np.broadcast_to(tw[:, None, :], (2, 8, HALF)).copy()
    row_tw = np.broadcast_to(tw[:, :, None], (2, HALF, HALF)).copy()
    order = np.zeros((PS, PS), np.float32)
    lane = np.arange(PS)
    order[lane, (lane % 2) * HALF + lane // 2] = 1.0
    orders = np.stack([order, order.T]).astype(ml_dtypes.bfloat16)
    return tables, lane_tw, row_tw, orders


def dot(left, right):
    return jnp.dot(left, right, preferred_element_type=F32)


def halves(x):
    high = x.astype(BF16)
    return high, (x - high.astype(F32)).astype(BF16)


def kernel(
    rows_n,
    cols_n,
    obj, probe, counts, offs, count, tables, lane_tw, row_tw, order,
    out_obj, out_probe,
    own, ext, patch, turned, measured, sorted_counts, probe_v, tab, ltw, rtw, perm,
    y_hi, y_lo, spec, grad, gsum, from_out, shared, core_in, plane_in, depth_in, final,
    load_sem, in_send, in_recv, fwd_send, out_send, out_recv,
    core_send, core_recv, plane_send, plane_recv, depth_send, depth_recv,
    spread_send, spread_recv, gather_send, gather_recv, last_send, last_recv,
):
    row, col = lax.axis_index("row"), lax.axis_index("col")
    core = lax.rem(row, 2)
    x_lo = lax.rem(row // 2, 2)
    y = row // 4
    z = col // 2
    x_hi = lax.rem(col, 2)
    depth = cols_n // 2
    rank = y * 4 + x_hi * 2 + x_lo

    def on_plane(other):
        return ((other // 4) * 4 + lax.rem(other, 2) * 2 + core, z * 2 + lax.rem(other // 2, 2))

    def at_depth(other):
        return (row, other * 2 + x_hi)

    up, down = lax.rem(row + rows_n - 1, rows_n), lax.rem(row + 1, rows_n)
    left, right = lax.rem(col + cols_n - 1, cols_n), lax.rem(col + 1, cols_n)
    partner = (row + 1 - 2 * core, col)
    even = core == 0

    barrier = pltpu.get_barrier_semaphore()
    known = [(row, left), (row, right), (up, col), (down, col)]
    for other in known:
        pl.semaphore_signal(barrier, inc=1, device_id=other, device_id_type=MESH)

    @pl.when(even)
    def _():
        pl.semaphore_signal(barrier, inc=1, device_id=(up, left), device_id_type=MESH)

    @pl.when(jnp.logical_not(even))
    def _():
        pl.semaphore_signal(barrier, inc=1, device_id=(down, right), device_id_type=MESH)

    for step in range(1, PLANE):
        pl.semaphore_signal(
            barrier, inc=1, device_id=on_plane(lax.rem(rank + step, PLANE)), device_id_type=MESH
        )
    for step in range(1, depth):
        pl.semaphore_signal(
            barrier, inc=1, device_id=at_depth(lax.rem(z + step, depth)), device_id_type=MESH
        )

    loads = []
    for index, (src, dst) in enumerate(
        [
            (obj, own), (probe, probe_v), (counts, measured), (tables, tab),
            (lane_tw, ltw), (row_tw, rtw), (order, perm),
        ]
    ):
        load = pltpu.make_async_copy(src, dst, load_sem.at[index])
        load.start()
        loads.append(load)

    pl.semaphore_wait(barrier, 5 + PLANE - 1 + depth - 1)

    def halo_copy(slot, chunk, target):
        part = pl.ds(chunk * ROWS, ROWS)
        return pltpu.make_async_remote_copy(
            src_ref=obj.at[:, part, :],
            dst_ref=ext.at[slot, :, part, :],
            send_sem=in_send.at[slot, chunk],
            recv_sem=in_recv.at[slot, chunk],
            device_id=target,
            device_id_type=MESH,
        )

    def forward_copy(chunk):
        part = pl.ds(chunk * ROWS, ROWS)
        return pltpu.make_async_remote_copy(
            src_ref=ext.at[0, :, part, :],
            dst_ref=ext.at[2, :, part, :],
            send_sem=fwd_send.at[chunk],
            recv_sem=in_recv.at[2, chunk],
            device_id=partner,
            device_id_type=MESH,
        )

    for chunk in range(CHUNKS):
        halo_copy(0, chunk, (row, left)).start()
        halo_copy(1, chunk, (up, col)).start()

        @pl.when(even)
        def _():
            halo_copy(2, chunk, (up, left)).start()

    for load in loads:
        load.wait()

    def prepare(slot, carry):
        oy, ox = offs[0, 0, slot, 0], offs[0, 0, slot, 1]
        for part in range(2):
            plane = pltpu.roll(probe_v[part], oy, 0)
            turned[slot, part] = pltpu.roll(plane, ox, 1)
        rest = measured[0, 0, slot]
        total = None
        for _ in range(3):
            piece = rest.astype(BF16)
            rest = rest - piece.astype(F32)
            piece = dot(dot(perm[1], piece).astype(BF16), perm[0])
            total = piece if total is None else total + piece
        sorted_counts[slot] = total
        return carry

    lax.fori_loop(0, CAP, prepare, 0)
    gsum[...] = jnp.zeros_like(gsum)
    grad[...] = jnp.zeros_like(grad)

    tw_re, tw_im = ltw[0, 0:1, :], ltw[1, 0:1, :]

    for chunk in range(CHUNKS):
        first_row = chunk * ROWS
        part = pl.ds(first_row, ROWS)
        for slot in range(2):
            halo_copy(slot, chunk, partner).wait_recv()

        @pl.when(jnp.logical_not(even))
        def _():
            forward_copy(chunk).start()

        halo_copy(2, chunk, partner).wait_recv()

        def enter(slot, carry):
            oy, ox = offs[0, 0, slot, 0], offs[0, 0, slot, 1]
            row_at = lax.broadcasted_iota(jnp.int32, (ROWS, PS), 0) + first_row
            lane_at = lax.broadcasted_iota(jnp.int32, (ROWS, PS), 1)
            is_own_row = row_at >= oy
            is_own_col = lane_at >= ox
            low_ok = row < rows_n - 1
            right_ok = col < cols_n - 1
            use_own = jnp.logical_and(is_own_row, is_own_col)
            use_right = jnp.logical_and(jnp.logical_and(is_own_row, ~is_own_col), right_ok)
            use_low = jnp.logical_and(jnp.logical_and(~is_own_row, is_own_col), low_ok)
            use_diag = jnp.logical_and(
                jnp.logical_and(~is_own_row, ~is_own_col), jnp.logical_and(low_ok, right_ok)
            )
            planes = []
            for p in range(2):
                value = jnp.where(use_own, own[p, part, :], 0.0)
                value = jnp.where(use_right, ext[0, p, part, :], value)
                value = jnp.where(use_low, ext[1, p, part, :], value)
                value = jnp.where(use_diag, ext[2, p, part, :], value)
                patch[slot, p, part, :] = value
                planes.append(value)
            pr, pi = turned[slot, 0, part, :], turned[slot, 1, part, :]
            er = pr * planes[0] - pi * planes[1]
            ei = pr * planes[1] + pi * planes[0]
            ar, br, ai, bi = er[:, :HALF], er[:, HALF:], ei[:, :HALF], ei[:, HALF:]
            dr, di = ar - br, ai - bi
            sums = jnp.concatenate([ar + br, ai + bi], axis=1)
            diffs = jnp.concatenate([dr * tw_re - di * tw_im, dr * tw_im + di * tw_re], axis=1)
            at = pl.ds(pl.multiple_of(slot * ROWS, ROWS), ROWS)
            for parity, value in enumerate((sums, diffs)):
                high, low = halves(value)
                y_hi[parity, at, :] = high
                y_lo[parity, at, :] = low
            return carry

        lax.fori_loop(0, CAP, enter, 0)
        for parity in range(2):
            value = (
                dot(y_hi[parity], tab[0]) + dot(y_lo[parity], tab[0]) + dot(y_hi[parity], tab[1])
            )
            for slot in range(CAP):
                spec[slot, parity, part, :] = value[slot * ROWS : (slot + 1) * ROWS]

    def position(slot, carry):
        oy, ox = offs[0, 0, slot, 0], offs[0, 0, slot, 1]
        valid = jnp.where(count[0, 0] > slot, 1.0, 0.0).astype(F32)
        cr = jnp.concatenate([rtw[0], rtw[0]], axis=1)
        ci = jnp.concatenate([rtw[1], rtw[1]], axis=1)

        def block(where, half):
            piece = spec[slot, :, where, half * HALF : (half + 1) * HALF]
            return jnp.concatenate([piece[0], piece[1]], axis=1)

        top, bottom = pl.ds(0, HALF), pl.ds(HALF, HALF)
        ar, ai, br, bi = block(top, 0), block(top, 1), block(bottom, 0), block(bottom, 1)
        dr, di = ar - br, ai - bi
        sums = jnp.concatenate([ar + br, ai + bi], axis=0)
        diffs = jnp.concatenate([dr * cr - di * ci, dr * ci + di * cr], axis=0)
        backs = []
        for parity, value in enumerate((sums, diffs)):
            high, low = halves(value)
            wave = dot(tab[2], high) + dot(tab[2], low) + dot(tab[3], high)
            wr, wi = wave[:HALF], wave[HALF:]
            model = wr * wr + wi * wi + 0.5
            guess = pl.reciprocal(model, approx=True)
            guess = guess * (2.0 - model * guess)
            seen = sorted_counts[slot, parity * HALF : (parity + 1) * HALF, :]
            weight = valid - (valid * seen) * guess
            weighted = jnp.concatenate([weight * wr, weight * wi], axis=0)
            high, low = halves(weighted)
            backs.append(dot(tab[0], high) + dot(tab[0], low) + dot(tab[1], high))
        er, ei = backs[0][:HALF], backs[0][HALF:]
        dr, di = backs[1][:HALF], backs[1][HALF:]
        fr, fi = dr * cr + di * ci, di * cr - dr * ci
        vr = jnp.concatenate([er + fr, er - fr], axis=0)
        vi = jnp.concatenate([ei + fi, ei - fi], axis=0)
        ends = []
        for parity in range(2):
            lanes = slice(parity * HALF, (parity + 1) * HALF)
            high, low = halves(jnp.concatenate([vr[:, lanes], vi[:, lanes]], axis=1))
            ends.append(dot(high, tab[2]) + dot(low, tab[2]) + dot(high, tab[3]))
        er, ei = ends[0][:, :HALF], ends[0][:, HALF:]
        dr, di = ends[1][:, :HALF], ends[1][:, HALF:]
        fr, fi = dr * tw_re + di * tw_im, di * tw_re - dr * tw_im
        chi_r = jnp.concatenate([er + fr, er - fr], axis=1)
        chi_i = jnp.concatenate([ei + fi, ei - fi], axis=1)

        pr, pi = patch[slot, 0], patch[slot, 1]
        back_y, back_x = lax.rem(PS - oy, PS), lax.rem(PS - ox, PS)
        for p, value in enumerate(
            (
                pr * chi_r + pi * chi_i,
                pr * chi_i - pi * chi_r,
                valid * (pr * pr + pi * pi),
            )
        ):
            value = pltpu.roll(pltpu.roll(value, back_y, 0), back_x, 1)
            gsum[2 * p] += value[:, :HALF]
            gsum[2 * p + 1] += value[:, HALF:]

        qr, qi = turned[slot, 0], turned[slot, 1]
        is_own_row = lax.broadcasted_iota(jnp.int32, (PS, PS), 0) >= oy
        is_own_col = lax.broadcasted_iota(jnp.int32, (PS, PS), 1) >= ox
        for p, value in enumerate((qr * chi_r + qi * chi_i, qr * chi_i - qi * chi_r)):
            here = jnp.where(is_own_col, value, 0.0)
            there = value - here
            here_own = jnp.where(is_own_row, here, 0.0)
            there_own = jnp.where(is_own_row, there, 0.0)
            grad[0, p] += here_own
            grad[1, p] += there_own
            grad[2, p] += here - here_own
            grad[3, p] += there - there_own
        return carry

    lax.fori_loop(0, CAP, position, 0)

    mine = pl.ds(pl.multiple_of(core * HALF, HALF), HALF)
    other = pl.ds(pl.multiple_of((1 - core) * HALF, HALF), HALF)

    def remote(src, dst, send, recv, target):
        return pltpu.make_async_remote_copy(
            src_ref=src, dst_ref=dst, send_sem=send, recv_sem=recv,
            device_id=target, device_id_type=MESH,
        )

    core_copy = remote(gsum.at[:, other, :], core_in, core_send, core_recv, partner)
    core_copy.start()

    share_copy = remote(grad.at[3], shared, out_send.at[3], out_recv.at[3], partner)
    low_copy = remote(grad.at[2], from_out.at[1], out_send.at[1], out_recv.at[1], (down, col))
    right_copy = remote(grad.at[1], from_out.at[0], out_send.at[0], out_recv.at[0], (row, right))
    diag_copy = remote(grad.at[3], from_out.at[2], out_send.at[2], out_recv.at[2], (down, right))

    @pl.when(even)
    def _():
        share_copy.start()

    low_copy.start()

    @pl.when(even)
    def _():
        right_copy.start()

    @pl.when(jnp.logical_not(even))
    def _():
        diag_copy.start()

    core_copy.wait_recv()
    core_in[...] = core_in[...] + gsum[:, mine, :]

    def plane_copy(step):
        target = lax.rem(rank + step, PLANE)
        rows8 = pl.ds(pl.multiple_of(target * 8, 8), 8)
        return remote(
            core_in.at[:, rows8, :], plane_in.at[step],
            plane_send.at[step], plane_recv.at[step], on_plane(target),
        )

    for step in range(1, PLANE):
        plane_copy(step).start()

    @pl.when(jnp.logical_not(even))
    def _():
        share_copy.wait_recv()
        grad[1] = grad[1] + shared[...]
        right_copy.start()

    mine8 = pl.ds(pl.multiple_of(rank * 8, 8), 8)
    total = core_in[:, mine8, :]
    for step in range(1, PLANE):
        plane_copy(step).wait_recv()
        total = total + plane_in[step]
    plane_in[0] = total

    shift = lax.rem(rank, OWNERS)
    stride = depth // OWNERS

    def depth_step(part):
        return lax.rem(z - (part * stride + lax.rem(shift, stride)) + depth, depth)

    def depth_copies(part):
        step = depth_step(part)
        target = at_depth(part * stride + lax.rem(shift, stride))
        return (
            remote(
                plane_in.at[0, part], depth_in.at[step, 0],
                depth_send.at[part, 0], depth_recv.at[step, 0], target,
            ),
            remote(
                plane_in.at[0, 4 + part % 2], depth_in.at[step, 1],
                depth_send.at[part, 1], depth_recv.at[step, 1], target,
            ),
        )

    for part in range(OWNERS):
        @pl.when(depth_step(part) != 0)
        def _():
            for copy in depth_copies(part):
                copy.start()

    my_part = z // stride
    is_owner = lax.rem(z, stride) == lax.rem(shift, stride)
    place = pl.ds(pl.multiple_of(core * HALF + rank * 8, 8), 8)

    def spread_copy(step):
        return remote(
            final.at[my_part, place, :], final.at[my_part, place, :],
            spread_send.at[step], spread_recv.at[my_part], at_depth(lax.rem(z + step, depth)),
        )

    for part in range(OWNERS):
        @pl.when(depth_step(part) == 0)
        def _():
            gradient = plane_in[0, part]
            light = plane_in[0, 4 + part % 2]
            for other_step in range(1, depth):
                for which in range(2):
                    remote(
                        plane_in.at[0, part], depth_in.at[other_step, which],
                        depth_send.at[part, which], depth_recv.at[other_step, which], partner,
                    ).wait_recv()
                gradient = gradient + depth_in[other_step, 0]
                light = light + depth_in[other_step, 1]
            final[part, place, :] = gradient * lax.rsqrt(light + 1.0)

    @pl.when(is_owner)
    def _():
        for step in range(1, depth):
            spread_copy(step).start()

    for part in range(OWNERS):
        @pl.when(depth_step(part) != 0)
        def _():
            remote(
                final.at[part, place, :], final.at[part, place, :],
                spread_send.at[0], spread_recv.at[part], partner,
            ).wait_recv()

    def gather_copy(step):
        return remote(
            final.at[:, place, :], final.at[:, place, :],
            gather_send.at[step], gather_recv.at[step], on_plane(lax.rem(rank + step, PLANE)),
        )

    def gather_arrival(step):
        source = lax.rem(rank + PLANE - step, PLANE)
        at = pl.ds(pl.multiple_of(core * HALF + source * 8, 8), 8)
        return remote(
            final.at[:, at, :], final.at[:, at, :],
            gather_send.at[step], gather_recv.at[step], partner,
        )

    for step in range(1, PLANE):
        gather_copy(step).start()
    for step in range(1, PLANE):
        gather_arrival(step).wait_recv()
    last_copy = remote(final.at[:, mine, :], final.at[:, mine, :], last_send, last_recv, partner)
    last_arrival = remote(final.at[:, other, :], final.at[:, other, :], last_send, last_recv, partner)
    last_copy.start()

    low_copy.wait_recv()
    right_copy.wait_recv()
    above = jnp.where(row > 0, 1.0, 0.0).astype(F32)
    before = jnp.where(col > 0, 1.0, 0.0).astype(F32)
    tile = grad[0] + before * from_out[0] + above * from_out[1]
    out_obj[...] = tile

    @pl.when(even)
    def _():
        diag_copy.wait_recv()
        out_obj[...] = out_obj[...] + (above * before) * from_out[2]

    last_arrival.wait_recv()
    for p in range(2):
        out_probe[p, :, :HALF] = final[2 * p]
        out_probe[p, :, HALF:] = final[2 * p + 1]

    for chunk in range(CHUNKS):
        halo_copy(0, chunk, partner).wait_send()
        halo_copy(1, chunk, partner).wait_send()

        @pl.when(even)
        def _():
            halo_copy(2, chunk, partner).wait_send()

        @pl.when(jnp.logical_not(even))
        def _():
            forward_copy(chunk).wait_send()

    core_copy.wait_send()
    low_copy.wait_send()
    right_copy.wait_send()

    @pl.when(even)
    def _():
        share_copy.wait_send()

    @pl.when(jnp.logical_not(even))
    def _():
        diag_copy.wait_send()

    for step in range(1, PLANE):
        plane_copy(step).wait_send()
        gather_copy(step).wait_send()
    for part in range(OWNERS):
        @pl.when(depth_step(part) != 0)
        def _():
            for copy in depth_copies(part):
                copy.wait_send()

    @pl.when(is_owner)
    def _():
        for step in range(1, depth):
            spread_copy(step).wait_send()

    last_copy.wait_send()


def on_device(rows_n, cols_n, object_field, probe, counts_measured, offsets, slot_count):
    tables, lane_tw, row_tw, order = constants()
    depth = cols_n // 2
    any_spec = pl.BlockSpec(memory_space=pl.ANY)
    smem_spec = pl.BlockSpec(memory_space=pltpu.SMEM)
    vmem_spec = pl.BlockSpec(memory_space=pltpu.VMEM)
    tile = (2, PS, PS)
    dma = pltpu.SemaphoreType.DMA
    return pl.pallas_call(
        functools.partial(kernel, rows_n, cols_n),
        out_shape=(jax.ShapeDtypeStruct(tile, F32), jax.ShapeDtypeStruct(tile, F32)),
        in_specs=[any_spec, any_spec, any_spec, smem_spec, smem_spec] + [any_spec] * 4,
        out_specs=(vmem_spec, vmem_spec),
        scratch_shapes=[
            pltpu.VMEM(tile, F32),
            pltpu.VMEM((3,) + tile, F32),
            pltpu.VMEM((CAP,) + tile, F32),
            pltpu.VMEM((CAP,) + tile, F32),
            pltpu.VMEM((1, 1, CAP, PS, PS), F32),
            pltpu.VMEM((CAP, PS, PS), F32),
            pltpu.VMEM(tile, F32),
            pltpu.VMEM((4, PS, PS), BF16),
            pltpu.VMEM((2, 8, HALF), F32),
            pltpu.VMEM((2, HALF, HALF), F32),
            pltpu.VMEM((2, PS, PS), BF16),
            pltpu.VMEM((2, CAP * ROWS, PS), BF16),
            pltpu.VMEM((2, CAP * ROWS, PS), BF16),
            pltpu.VMEM((CAP, 2, PS, PS), F32),
            pltpu.VMEM((4,) + tile, F32),
            pltpu.VMEM((6, PS, HALF), F32),
            pltpu.VMEM((3,) + tile, F32),
            pltpu.VMEM(tile, F32),
            pltpu.VMEM((6, HALF, HALF), F32),
            pltpu.VMEM((PLANE, 6, 8, HALF), F32),
            pltpu.VMEM((depth, 2, 8, HALF), F32),
            pltpu.VMEM((4, PS, HALF), F32),
            dma((7,)),
            dma((3, CHUNKS)),
            dma((3, CHUNKS)),
            dma((CHUNKS,)),
            dma((4,)),
            dma((4,)),
            dma,
            dma,
            dma((PLANE,)),
            dma((PLANE,)),
            dma((OWNERS, 2)),
            dma((depth, 2)),
            dma((depth,)),
            dma((OWNERS,)),
            dma((PLANE,)),
            dma((PLANE,)),
            dma,
            dma,
        ],
        compiler_params=pltpu.CompilerParams(
            collective_id=0, has_side_effects=True, vmem_limit_bytes=48 << 20
        ),
        name="ptychography",
    )(
        object_field, probe, counts_measured, offsets, slot_count,
        jnp.asarray(tables), jnp.asarray(lane_tw), jnp.asarray(row_tw), jnp.asarray(order),
    )


def solution(mesh):
    rows_n, cols_n = mesh.shape["row"], mesh.shape["col"]
    return jax.shard_map(
        functools.partial(on_device, rows_n, cols_n),
        mesh=mesh,
        in_specs=(
            P(None, "row", "col"),
            P(),
            P("row", "col", None, None, None),
            P("row", "col", None, None),
            P("row", "col"),
        ),
        out_specs=(P(None, "row", "col"), P()),
        check_vma=False,
    )
```

```python
import functools
import math

import jax
import jax.numpy as jnp
import numpy as np
from jax import lax
from jax.experimental import pallas as pl
from jax.experimental.pallas import tpu as pltpu
from jax.sharding import PartitionSpec as P

MESH = pl.DeviceIdType.MESH
PS = 256
HALF = 128
CAP = 4
CHUNKS = 4
ROWS = PS // CHUNKS
PLANE = 16
NEAR = 4
F32 = jnp.float32
BF16 = jnp.bfloat16


def constants():
    n = np.arange(HALF)
    angle = 2.0 * math.pi * ((n[:, None] * n[None, :]) % HALF) / HALF
    cos, sin = np.cos(angle) / 16.0, np.sin(angle) / 16.0
    matrix = np.block([[cos, -sin], [sin, cos]])
    tables = np.stack([matrix, matrix.T]).astype(np.float32)
    turn = 2.0 * math.pi * n / PS
    tw = np.stack([np.cos(turn), -np.sin(turn)]).astype(np.float32)
    lane_tw = np.broadcast_to(tw[:, None, :], (2, 8, HALF)).copy()
    row_tw = np.broadcast_to(tw[:, :, None], (2, HALF, HALF)).copy()
    order = np.zeros((PS, PS), np.float32)
    lane = np.arange(PS)
    order[lane, (lane % 2) * HALF + lane // 2] = 1.0
    orders = np.stack([order, order.T])
    return np.concatenate([tables, orders]), lane_tw, row_tw


def dot(left, right):
    return jnp.dot(left, right, preferred_element_type=F32)


def halves(x):
    high = x.astype(BF16)
    return high, (x - high.astype(F32)).astype(BF16)


def kernel(
    rows_n,
    cols_n,
    obj, probe, counts, offs, count, tables, lane_tw, row_tw,
    out_obj, out_probe,
    own, ext, patch, turned, measured, sorted_counts, probe_v, made, tab, ltw, rtw, perm,
    y_hi, y_lo, spec, grad, gsum, lsum, from_out, shared, final,
    core_in, plane_in, near_in, far_in, core_light, plane_light, near_light, far_light,
    load_sem, in_send, in_recv, fwd_send, out_send, out_recv,
    core_send, core_recv, plane_send, plane_recv, near_send, near_recv, far_send, far_recv,
    gather_send, gather_recv, last_send, last_recv, store_sem,
):
    row, col = lax.axis_index("row"), lax.axis_index("col")
    core = lax.rem(row, 2)
    x_lo = lax.rem(row // 2, 2)
    y = row // 4
    z = col // 2
    x_hi = lax.rem(col, 2)
    rank = y * 4 + x_hi * 2 + x_lo

    def on_plane(other):
        return ((other // 4) * 4 + lax.rem(other, 2) * 2 + core, z * 2 + lax.rem(other // 2, 2))

    def at_depth(other):
        return (row, other * 2 + x_hi)

    group, member = z // NEAR, lax.rem(z, NEAR)

    def near(step):
        return group * NEAR + lax.rem(member + step, NEAR)

    def far(step):
        return lax.rem(group + step, NEAR) * NEAR + member

    up, down = lax.rem(row + rows_n - 1, rows_n), lax.rem(row + 1, rows_n)
    left, right = lax.rem(col + cols_n - 1, cols_n), lax.rem(col + 1, cols_n)
    partner = (row + 1 - 2 * core, col)
    even = core == 0

    barrier = pltpu.get_barrier_semaphore()
    known = [(row, left), (row, right), (up, col), (down, col)]
    for other in known:
        pl.semaphore_signal(barrier, inc=1, device_id=other, device_id_type=MESH)

    @pl.when(even)
    def _():
        pl.semaphore_signal(barrier, inc=1, device_id=(up, left), device_id_type=MESH)

    @pl.when(jnp.logical_not(even))
    def _():
        pl.semaphore_signal(barrier, inc=1, device_id=(down, right), device_id_type=MESH)

    for step in range(1, PLANE):
        pl.semaphore_signal(
            barrier, inc=1, device_id=on_plane(lax.rem(rank + step, PLANE)), device_id_type=MESH
        )
    for step in range(1, NEAR):
        for other in (near(step), far(step)):
            pl.semaphore_signal(barrier, inc=1, device_id=at_depth(other), device_id_type=MESH)

    loads = []
    for index, (src, dst) in enumerate(
        [
            (obj, own), (probe, probe_v), (counts, measured), (tables, made),
            (lane_tw, ltw), (row_tw, rtw),
        ]
    ):
        load = pltpu.make_async_copy(src, dst, load_sem.at[index])
        load.start()
        loads.append(load)

    pl.semaphore_wait(barrier, 5 + PLANE - 1 + 2 * (NEAR - 1))

    def halo_copy(slot, chunk, target):
        part = pl.ds(chunk * ROWS, ROWS)
        return pltpu.make_async_remote_copy(
            src_ref=obj.at[:, part, :],
            dst_ref=ext.at[slot, :, part, :],
            send_sem=in_send.at[slot, chunk],
            recv_sem=in_recv.at[slot, chunk],
            device_id=target,
            device_id_type=MESH,
        )

    def forward_copy(chunk):
        part = pl.ds(chunk * ROWS, ROWS)
        return pltpu.make_async_remote_copy(
            src_ref=ext.at[0, :, part, :],
            dst_ref=ext.at[2, :, part, :],
            send_sem=fwd_send.at[chunk],
            recv_sem=in_recv.at[2, chunk],
            device_id=partner,
            device_id_type=MESH,
        )

    for chunk in range(CHUNKS):
        halo_copy(0, chunk, (row, left)).start()
        halo_copy(1, chunk, (up, col)).start()

        @pl.when(even)
        def _():
            halo_copy(2, chunk, (up, left)).start()

    for load in loads:
        load.wait()

    for index in range(2):
        tab[2 * index], tab[2 * index + 1] = halves(made[index])
        perm[index] = made[2 + index].astype(BF16)

    def prepare(slot, carry):
        oy, ox = offs[0, 0, 0, slot], offs[0, 0, 1, slot]
        for part in range(2):
            plane = pltpu.roll(probe_v[part], oy, 0)
            turned[slot, part] = pltpu.roll(plane, ox, 1)
        rest = measured[0, 0, slot]
        total = None
        for _ in range(3):
            piece = rest.astype(BF16)
            rest = rest - piece.astype(F32)
            piece = dot(dot(perm[1], piece).astype(BF16), perm[0])
            total = piece if total is None else total + piece
        sorted_counts[slot] = total
        return carry

    lax.fori_loop(0, CAP, prepare, 0)
    gsum[...] = jnp.zeros_like(gsum)
    lsum[...] = jnp.zeros_like(lsum)
    grad[...] = jnp.zeros_like(grad)

    tw_re, tw_im = ltw[0, 0:1, :], ltw[1, 0:1, :]

    for chunk in range(CHUNKS):
        first_row = chunk * ROWS
        part = pl.ds(first_row, ROWS)
        for slot in range(2):
            halo_copy(slot, chunk, partner).wait_recv()

        @pl.when(jnp.logical_not(even))
        def _():
            forward_copy(chunk).start()

        halo_copy(2, chunk, partner).wait_recv()

        def enter(slot, carry):
            oy, ox = offs[0, 0, 0, slot], offs[0, 0, 1, slot]
            row_at = lax.broadcasted_iota(jnp.int32, (ROWS, PS), 0) + first_row
            lane_at = lax.broadcasted_iota(jnp.int32, (ROWS, PS), 1)
            is_own_row = row_at >= oy
            is_own_col = lane_at >= ox
            low_ok = row < rows_n - 1
            right_ok = col < cols_n - 1
            use_own = jnp.logical_and(is_own_row, is_own_col)
            use_right = jnp.logical_and(jnp.logical_and(is_own_row, ~is_own_col), right_ok)
            use_low = jnp.logical_and(jnp.logical_and(~is_own_row, is_own_col), low_ok)
            use_diag = jnp.logical_and(
                jnp.logical_and(~is_own_row, ~is_own_col), jnp.logical_and(low_ok, right_ok)
            )
            planes = []
            for p in range(2):
                value = jnp.where(use_own, own[p, part, :], 0.0)
                value = jnp.where(use_right, ext[0, p, part, :], value)
                value = jnp.where(use_low, ext[1, p, part, :], value)
                value = jnp.where(use_diag, ext[2, p, part, :], value)
                patch[slot, p, part, :] = value
                planes.append(value)
            pr, pi = turned[slot, 0, part, :], turned[slot, 1, part, :]
            er = pr * planes[0] - pi * planes[1]
            ei = pr * planes[1] + pi * planes[0]
            ar, br, ai, bi = er[:, :HALF], er[:, HALF:], ei[:, :HALF], ei[:, HALF:]
            dr, di = ar - br, ai - bi
            sums = jnp.concatenate([ar + br, ai + bi], axis=1)
            diffs = jnp.concatenate([dr * tw_re - di * tw_im, dr * tw_im + di * tw_re], axis=1)
            at = pl.ds(pl.multiple_of(slot * ROWS, ROWS), ROWS)
            for parity, value in enumerate((sums, diffs)):
                high, low = halves(value)
                y_hi[parity, at, :] = high
                y_lo[parity, at, :] = low
            return carry

        lax.fori_loop(0, CAP, enter, 0)
        for parity in range(2):
            value = (
                dot(y_hi[parity], tab[0]) + dot(y_lo[parity], tab[0]) + dot(y_hi[parity], tab[1])
            )
            for slot in range(CAP):
                spec[slot, parity, part, :] = value[slot * ROWS : (slot + 1) * ROWS]

    def position(slot, carry):
        oy, ox = offs[0, 0, 0, slot], offs[0, 0, 1, slot]
        valid = jnp.where(count[0, 0] > slot, 1.0, 0.0).astype(F32)
        cr = jnp.concatenate([rtw[0], rtw[0]], axis=1)
        ci = jnp.concatenate([rtw[1], rtw[1]], axis=1)

        def block(where, half):
            piece = spec[slot, :, where, half * HALF : (half + 1) * HALF]
            return jnp.concatenate([piece[0], piece[1]], axis=1)

        top, bottom = pl.ds(0, HALF), pl.ds(HALF, HALF)
        ar, ai, br, bi = block(top, 0), block(top, 1), block(bottom, 0), block(bottom, 1)
        dr, di = ar - br, ai - bi
        sums = jnp.concatenate([ar + br, ai + bi], axis=0)
        diffs = jnp.concatenate([dr * cr - di * ci, dr * ci + di * cr], axis=0)
        backs = []
        for parity, value in enumerate((sums, diffs)):
            high, low = halves(value)
            wave = dot(tab[2], high) + dot(tab[2], low) + dot(tab[3], high)
            wr, wi = wave[:HALF], wave[HALF:]
            model = wr * wr + wi * wi + 0.5
            guess = pl.reciprocal(model, approx=True)
            guess = guess * (2.0 - model * guess)
            seen = sorted_counts[slot, parity * HALF : (parity + 1) * HALF, :]
            weight = valid - (valid * seen) * guess
            weighted = jnp.concatenate([weight * wr, weight * wi], axis=0)
            high, low = halves(weighted)
            backs.append(dot(tab[0], high) + dot(tab[0], low) + dot(tab[1], high))
        er, ei = backs[0][:HALF], backs[0][HALF:]
        dr, di = backs[1][:HALF], backs[1][HALF:]
        fr, fi = dr * cr + di * ci, di * cr - dr * ci
        vr = jnp.concatenate([er + fr, er - fr], axis=0)
        vi = jnp.concatenate([ei + fi, ei - fi], axis=0)
        ends = []
        for parity in range(2):
            lanes = slice(parity * HALF, (parity + 1) * HALF)
            high, low = halves(jnp.concatenate([vr[:, lanes], vi[:, lanes]], axis=1))
            ends.append(dot(high, tab[2]) + dot(low, tab[2]) + dot(high, tab[3]))
        er, ei = ends[0][:, :HALF], ends[0][:, HALF:]
        dr, di = ends[1][:, :HALF], ends[1][:, HALF:]
        fr, fi = dr * tw_re + di * tw_im, di * tw_re - dr * tw_im
        chi_r = jnp.concatenate([er + fr, er - fr], axis=1)
        chi_i = jnp.concatenate([ei + fi, ei - fi], axis=1)

        pr, pi = patch[slot, 0], patch[slot, 1]
        back_y, back_x = lax.rem(PS - oy, PS), lax.rem(PS - ox, PS)
        for p, value in enumerate((pr * chi_r + pi * chi_i, pr * chi_i - pi * chi_r)):
            value = pltpu.roll(pltpu.roll(value, back_y, 0), back_x, 1)
            gsum[2 * p] += value[:, :HALF]
            gsum[2 * p + 1] += value[:, HALF:]

        spec[slot, 0] = chi_r
        spec[slot, 1] = chi_i
        return carry

    mine = pl.ds(pl.multiple_of(core * HALF, HALF), HALF)
    other = pl.ds(pl.multiple_of((1 - core) * HALF, HALF), HALF)
    mine8 = pl.ds(pl.multiple_of(rank * 8, 8), 8)
    place = pl.ds(pl.multiple_of(core * HALF + rank * 8, 8), 8)

    def remote(src, dst, send, recv, target):
        return pltpu.make_async_remote_copy(
            src_ref=src, dst_ref=dst, send_sem=send, recv_sem=recv,
            device_id=target, device_id_type=MESH,
        )

    class Sum:
        def __init__(self, full, core_in, plane_in, near_in, far_in, sems, which):
            self.full, self.core_in, self.plane_in = full, core_in, plane_in
            self.near_in, self.far_in = near_in, far_in
            (self.core_s, self.core_r, self.plane_s, self.plane_r,
             self.near_s, self.near_r, self.far_s, self.far_r) = sems
            self.which = which

        def core_copy(self):
            return remote(
                self.full.at[:, other, :], self.core_in,
                self.core_s.at[self.which], self.core_r.at[self.which], partner,
            )

        def plane_copy(self, step):
            target = lax.rem(rank + step, PLANE)
            rows8 = pl.ds(pl.multiple_of(target * 8, 8), 8)
            return remote(
                self.core_in.at[:, rows8, :], self.plane_in.at[step],
                self.plane_s.at[self.which, step], self.plane_r.at[self.which, step], on_plane(target),
            )

        def near_copy(self, step):
            return remote(
                self.near_in.at[member], self.near_in.at[member],
                self.near_s.at[self.which, step], self.near_r.at[self.which, step], at_depth(near(step)),
            )

        def near_arrival(self, step):
            at = lax.rem(member + NEAR - step, NEAR)
            return remote(
                self.near_in.at[at], self.near_in.at[at],
                self.near_s.at[self.which, step], self.near_r.at[self.which, step], partner,
            )

        def far_copy(self, step):
            return remote(
                self.far_in.at[group], self.far_in.at[group],
                self.far_s.at[self.which, step], self.far_r.at[self.which, step], at_depth(far(step)),
            )

        def far_arrival(self, step):
            at = lax.rem(group + NEAR - step, NEAR)
            return remote(
                self.far_in.at[at], self.far_in.at[at],
                self.far_s.at[self.which, step], self.far_r.at[self.which, step], partner,
            )

        def start(self):
            self.core_copy().start()

        def over_plane(self):
            self.core_copy().wait_recv()
            self.core_in[...] = self.core_in[...] + self.full[:, mine, :]
            for step in range(1, PLANE):
                self.plane_copy(step).start()

        def over_near(self):
            total = self.core_in[:, mine8, :]
            for step in range(1, PLANE):
                self.plane_copy(step).wait_recv()
                total = total + self.plane_in[step]
            self.near_in[member] = total
            for step in range(1, NEAR):
                self.near_copy(step).start()

        def over_far(self):
            for step in range(1, NEAR):
                self.near_arrival(step).wait_recv()
            self.far_in[group] = (self.near_in[0] + self.near_in[1]) + (self.near_in[2] + self.near_in[3])
            for step in range(1, NEAR):
                self.far_copy(step).start()

        def result(self):
            for step in range(1, NEAR):
                self.far_arrival(step).wait_recv()
            return (self.far_in[0] + self.far_in[1]) + (self.far_in[2] + self.far_in[3])

        def wait_sent(self):
            self.core_copy().wait_send()
            for step in range(1, PLANE):
                self.plane_copy(step).wait_send()
            for step in range(1, NEAR):
                self.near_copy(step).wait_send()
                self.far_copy(step).wait_send()

    sums = (core_send, core_recv, plane_send, plane_recv, near_send, near_recv, far_send, far_recv)
    light = Sum(lsum, core_light, plane_light, near_light, far_light, sums, 1)
    terms = Sum(gsum, core_in, plane_in, near_in, far_in, sums, 0)

    def brighten(slot, carry):
        oy, ox = offs[0, 0, 0, slot], offs[0, 0, 1, slot]
        valid = jnp.where(count[0, 0] > slot, 1.0, 0.0).astype(F32)
        pr, pi = patch[slot, 0], patch[slot, 1]
        back_y, back_x = lax.rem(PS - oy, PS), lax.rem(PS - ox, PS)
        value = pltpu.roll(pltpu.roll(valid * (pr * pr + pi * pi), back_y, 0), back_x, 1)
        lsum[0] += value[:, :HALF]
        lsum[1] += value[:, HALF:]
        return carry

    lax.fori_loop(0, CAP, brighten, 0)
    light.start()

    def step_of(slot, carry):
        position(slot, carry)

        @pl.when(slot == 1)
        def _():
            light.over_plane()

        return carry

    lax.fori_loop(0, CAP, step_of, 0)
    terms.start()

    def place_out(slot, carry):
        oy, ox = offs[0, 0, 0, slot], offs[0, 0, 1, slot]
        chi_r, chi_i = spec[slot, 0], spec[slot, 1]
        qr, qi = turned[slot, 0], turned[slot, 1]
        is_own_row = lax.broadcasted_iota(jnp.int32, (PS, PS), 0) >= oy
        is_own_col = lax.broadcasted_iota(jnp.int32, (PS, PS), 1) >= ox
        for p, value in enumerate((qr * chi_r + qi * chi_i, qr * chi_i - qi * chi_r)):
            here = jnp.where(is_own_col, value, 0.0)
            there = value - here
            here_own = jnp.where(is_own_row, here, 0.0)
            there_own = jnp.where(is_own_row, there, 0.0)
            grad[0, p] += here_own
            grad[1, p] += there_own
            grad[2, p] += here - here_own
            grad[3, p] += there - there_own
        return carry

    lax.fori_loop(0, CAP, place_out, 0)

    share_copy = remote(grad.at[3], shared, out_send.at[3, 0], out_recv.at[3, 0], partner)
    low_copy = remote(grad.at[2], from_out.at[1], out_send.at[1, 0], out_recv.at[1, 0], (down, col))

    def out_copy(tile, slot, piece, target):
        part = pl.ds(piece * ROWS, ROWS)
        return remote(
            grad.at[tile, :, part, :], from_out.at[slot, :, part, :],
            out_send.at[slot, piece], out_recv.at[slot, piece], target,
        )

    def right_copy(piece):
        return out_copy(1, 0, piece, (row, right))

    def diag_copy(piece):
        return out_copy(3, 2, piece, (down, right))

    inner = x_hi == 0

    def leave(who, right_pieces, diag_pieces):
        @pl.when(who)
        def _():
            for piece in diag_pieces:
                diag_copy(piece).start()
            for piece in right_pieces:
                right_copy(piece).start()

    outer_even = jnp.logical_and(jnp.logical_not(inner), even)
    outer_odd = jnp.logical_and(jnp.logical_not(inner), jnp.logical_not(even))
    inner_even = jnp.logical_and(inner, even)
    inner_odd = jnp.logical_and(inner, jnp.logical_not(even))

    @pl.when(even)
    def _():
        share_copy.start()

    leave(outer_even, (0, 1), ())
    leave(outer_odd, (), (0, 1))
    terms.over_plane()
    light.over_near()
    low_copy.start()

    @pl.when(jnp.logical_not(even))
    def _():
        share_copy.wait_recv()
        grad[1] = grad[1] + shared[...]

    leave(inner_even, range(4), ())
    leave(inner_odd, range(4), range(4))
    terms.over_near()
    light.over_far()
    leave(outer_even, (2,), ())
    leave(outer_odd, (), (2, 3))
    terms.over_far()
    leave(outer_even, (3,), ())
    leave(outer_odd, range(4), ())
    bright = light.result()
    scale = lax.rsqrt(bright + 1.0)
    total = terms.result()
    final[0, place, :] = total[0] * scale[0]
    final[1, place, :] = total[1] * scale[1]
    final[2, place, :] = total[2] * scale[0]
    final[3, place, :] = total[3] * scale[1]

    def gather_copy(step):
        return remote(
            final.at[:, place, :], final.at[:, place, :],
            gather_send.at[step], gather_recv.at[step], on_plane(lax.rem(rank + step, PLANE)),
        )

    def gather_arrival(step):
        source = lax.rem(rank + PLANE - step, PLANE)
        at = pl.ds(pl.multiple_of(core * HALF + source * 8, 8), 8)
        return remote(
            final.at[:, at, :], final.at[:, at, :],
            gather_send.at[step], gather_recv.at[step], partner,
        )

    def store_probe(where, first):
        return [
            pltpu.make_async_copy(
                final.at[block, where, :],
                out_probe.at[block // 2, where, (block % 2) * HALF : (block % 2 + 1) * HALF],
                store_sem.at[first + block],
            )
            for block in range(4)
        ]

    for step in range(1, PLANE):
        gather_copy(step).start()
    for step in range(1, PLANE):
        gather_arrival(step).wait_recv()
    last_copy = remote(final.at[:, mine, :], final.at[:, mine, :], last_send, last_recv, partner)
    last_arrival = remote(final.at[:, other, :], final.at[:, other, :], last_send, last_recv, partner)
    last_copy.start()
    stores = store_probe(mine, 0)
    for store in stores:
        store.start()

    low_copy.wait_recv()
    for piece in range(4):
        right_copy(piece).wait_recv()
    above = jnp.where(row > 0, 1.0, 0.0).astype(F32)
    before = jnp.where(col > 0, 1.0, 0.0).astype(F32)
    own[...] = grad[0] + before * from_out[0] + above * from_out[1]

    @pl.when(even)
    def _():
        for piece in range(4):
            diag_copy(piece).wait_recv()
        own[...] = own[...] + (above * before) * from_out[2]

    store_tile = pltpu.make_async_copy(own, out_obj, store_sem.at[8])
    store_tile.start()
    last_arrival.wait_recv()
    rest = store_probe(other, 4)
    for store in rest:
        store.start()

    for chunk in range(CHUNKS):
        halo_copy(0, chunk, partner).wait_send()
        halo_copy(1, chunk, partner).wait_send()

        @pl.when(even)
        def _():
            halo_copy(2, chunk, partner).wait_send()

        @pl.when(jnp.logical_not(even))
        def _():
            forward_copy(chunk).wait_send()

    light.wait_sent()
    terms.wait_sent()
    low_copy.wait_send()
    for piece in range(4):
        right_copy(piece).wait_send()

    @pl.when(even)
    def _():
        share_copy.wait_send()

    @pl.when(jnp.logical_not(even))
    def _():
        for piece in range(4):
            diag_copy(piece).wait_send()

    for step in range(1, PLANE):
        gather_copy(step).wait_send()
    last_copy.wait_send()
    for store in stores + rest:
        store.wait()
    store_tile.wait()


def on_device(rows_n, cols_n, object_field, probe, counts_measured, offsets, slot_count):
    tables, lane_tw, row_tw = constants()
    any_spec = pl.BlockSpec(memory_space=pltpu.HBM)
    smem_spec = pl.BlockSpec(memory_space=pltpu.SMEM)
    tile = (2, PS, PS)
    dma = pltpu.SemaphoreType.DMA
    return pl.pallas_call(
        functools.partial(kernel, rows_n, cols_n),
        out_shape=(jax.ShapeDtypeStruct(tile, F32), jax.ShapeDtypeStruct(tile, F32)),
        in_specs=[any_spec, any_spec, any_spec, smem_spec, smem_spec] + [any_spec] * 3,
        out_specs=(any_spec, any_spec),
        scratch_shapes=[
            pltpu.VMEM(tile, F32),
            pltpu.VMEM((3,) + tile, F32),
            pltpu.VMEM((CAP,) + tile, F32),
            pltpu.VMEM((CAP,) + tile, F32),
            pltpu.VMEM((1, 1, CAP, PS, PS), F32),
            pltpu.VMEM((CAP, PS, PS), F32),
            pltpu.VMEM(tile, F32),
            pltpu.VMEM((4, PS, PS), F32),
            pltpu.VMEM((4, PS, PS), BF16),
            pltpu.VMEM((2, 8, HALF), F32),
            pltpu.VMEM((2, HALF, HALF), F32),
            pltpu.VMEM((2, PS, PS), BF16),
            pltpu.VMEM((2, CAP * ROWS, PS), BF16),
            pltpu.VMEM((2, CAP * ROWS, PS), BF16),
            pltpu.VMEM((CAP, 2, PS, PS), F32),
            pltpu.VMEM((4,) + tile, F32),
            pltpu.VMEM((4, PS, HALF), F32),
            pltpu.VMEM((2, PS, HALF), F32),
            pltpu.VMEM((3,) + tile, F32),
            pltpu.VMEM(tile, F32),
            pltpu.VMEM((4, PS, HALF), F32),
            pltpu.VMEM((4, HALF, HALF), F32),
            pltpu.VMEM((PLANE, 4, 8, HALF), F32),
            pltpu.VMEM((NEAR, 4, 8, HALF), F32),
            pltpu.VMEM((NEAR, 4, 8, HALF), F32),
            pltpu.VMEM((2, HALF, HALF), F32),
            pltpu.VMEM((PLANE, 2, 8, HALF), F32),
            pltpu.VMEM((NEAR, 2, 8, HALF), F32),
            pltpu.VMEM((NEAR, 2, 8, HALF), F32),
            dma((6,)),
            dma((3, CHUNKS)),
            dma((3, CHUNKS)),
            dma((CHUNKS,)),
            dma((4, 4)),
            dma((4, 4)),
            dma((2,)),
            dma((2,)),
            dma((2, PLANE)),
            dma((2, PLANE)),
            dma((2, NEAR)),
            dma((2, NEAR)),
            dma((2, NEAR)),
            dma((2, NEAR)),
            dma((PLANE,)),
            dma((PLANE,)),
            dma,
            dma,
            dma((9,)),
        ],
        compiler_params=pltpu.CompilerParams(
            collective_id=0, has_side_effects=True, vmem_limit_bytes=60 << 20
        ),
        name="ptychography",
    )(
        object_field, probe, counts_measured, jnp.swapaxes(offsets, 2, 3), slot_count,
        jnp.asarray(tables), jnp.asarray(lane_tw), jnp.asarray(row_tw),
    )


def solution(mesh):
    rows_n, cols_n = mesh.shape["row"], mesh.shape["col"]
    return jax.shard_map(
        functools.partial(on_device, rows_n, cols_n),
        mesh=mesh,
        in_specs=(
            P(None, "row", "col"),
            P(),
            P("row", "col", None, None, None),
            P("row", "col", None, None),
            P("row", "col"),
        ),
        out_specs=(P(None, "row", "col"), P()),
        check_vma=False,
    )
```

```python
import functools
import math

import jax
import jax.numpy as jnp
import numpy as np
from jax import lax
from jax.experimental import pallas as pl
from jax.experimental.pallas import tpu as pltpu
from jax.sharding import PartitionSpec as P

MESH = pl.DeviceIdType.MESH
PS = 256
HALF = 128
CAP = 4
CHUNKS = 4
ROWS = PS // CHUNKS
PLANE = 16
NEAR = 4
F32 = jnp.float32
BF16 = jnp.bfloat16


def constants():
    n = np.arange(HALF)
    angle = 2.0 * math.pi * ((n[:, None] * n[None, :]) % HALF) / HALF
    cos, sin = np.cos(angle) / 16.0, np.sin(angle) / 16.0
    matrix = np.block([[cos, -sin], [sin, cos]])
    tables = np.stack([matrix, matrix.T]).astype(np.float32)
    turn = 2.0 * math.pi * n / PS
    tw = np.stack([np.cos(turn), -np.sin(turn)]).astype(np.float32)
    lane_tw = np.broadcast_to(tw[:, None, :], (2, 8, HALF)).copy()
    row_tw = np.broadcast_to(tw[:, :, None], (2, HALF, HALF)).copy()
    order = np.zeros((PS, PS), np.float32)
    lane = np.arange(PS)
    order[lane, (lane % 2) * HALF + lane // 2] = 1.0
    orders = np.stack([order, order.T])
    return np.concatenate([tables, orders]), lane_tw, row_tw


def dot(left, right):
    return jnp.dot(left, right, preferred_element_type=F32)


def halves(x):
    high = x.astype(BF16)
    return high, (x - high.astype(F32)).astype(BF16)


def kernel(
    rows_n,
    cols_n,
    obj, probe, counts, offs, count, tables, lane_tw, row_tw,
    out_obj, out_probe,
    own, ext, patch, turned, measured, sorted_counts, probe_v, made, tab, ltw, rtw, perm,
    y_hi, y_lo, spec, twice, bright_twice, grad, gsum, lsum, from_out, shared, final,
    core_in, plane_in, near_in, far_in, core_light, plane_light, near_light, far_light,
    load_sem, in_send, in_recv, fwd_send, out_send, out_recv,
    core_send, core_recv, plane_send, plane_recv, near_send, near_recv, far_send, far_recv,
    gather_send, gather_recv, last_send, last_recv, store_sem,
):
    row, col = lax.axis_index("row"), lax.axis_index("col")
    core = lax.rem(row, 2)
    x_lo = lax.rem(row // 2, 2)
    y = row // 4
    z = col // 2
    x_hi = lax.rem(col, 2)
    rank = y * 4 + x_hi * 2 + x_lo

    def on_plane(other):
        return ((other // 4) * 4 + lax.rem(other, 2) * 2 + core, z * 2 + lax.rem(other // 2, 2))

    def at_depth(other):
        return (row, other * 2 + x_hi)

    group, member = z // NEAR, lax.rem(z, NEAR)

    def near(step):
        return group * NEAR + lax.rem(member + step, NEAR)

    def far(step):
        return lax.rem(group + step, NEAR) * NEAR + member

    up, down = lax.rem(row + rows_n - 1, rows_n), lax.rem(row + 1, rows_n)
    left, right = lax.rem(col + cols_n - 1, cols_n), lax.rem(col + 1, cols_n)
    partner = (row + 1 - 2 * core, col)
    even = core == 0

    barrier = pltpu.get_barrier_semaphore()
    known = [(row, left), (row, right), (up, col), (down, col)]
    for other in known:
        pl.semaphore_signal(barrier, inc=1, device_id=other, device_id_type=MESH)

    @pl.when(even)
    def _():
        pl.semaphore_signal(barrier, inc=1, device_id=(up, left), device_id_type=MESH)

    @pl.when(jnp.logical_not(even))
    def _():
        pl.semaphore_signal(barrier, inc=1, device_id=(down, right), device_id_type=MESH)

    for step in range(1, PLANE):
        pl.semaphore_signal(
            barrier, inc=1, device_id=on_plane(lax.rem(rank + step, PLANE)), device_id_type=MESH
        )
    for step in range(1, NEAR):
        for other in (near(step), far(step)):
            pl.semaphore_signal(barrier, inc=1, device_id=at_depth(other), device_id_type=MESH)

    loads = []
    for index, (src, dst) in enumerate(
        [
            (obj, own), (probe, probe_v), (counts, measured), (tables, made),
            (lane_tw, ltw), (row_tw, rtw),
        ]
    ):
        load = pltpu.make_async_copy(src, dst, load_sem.at[index])
        load.start()
        loads.append(load)

    pl.semaphore_wait(barrier, 5 + PLANE - 1 + 2 * (NEAR - 1))

    def halo_copy(slot, chunk, target):
        part = pl.ds(chunk * ROWS, ROWS)
        return pltpu.make_async_remote_copy(
            src_ref=obj.at[:, part, :],
            dst_ref=ext.at[slot, :, part, :],
            send_sem=in_send.at[slot, chunk],
            recv_sem=in_recv.at[slot, chunk],
            device_id=target,
            device_id_type=MESH,
        )

    def forward_copy(chunk):
        part = pl.ds(chunk * ROWS, ROWS)
        return pltpu.make_async_remote_copy(
            src_ref=ext.at[0, :, part, :],
            dst_ref=ext.at[2, :, part, :],
            send_sem=fwd_send.at[chunk],
            recv_sem=in_recv.at[2, chunk],
            device_id=partner,
            device_id_type=MESH,
        )

    for chunk in range(CHUNKS):
        halo_copy(0, chunk, (row, left)).start()
        halo_copy(1, chunk, (up, col)).start()

        @pl.when(even)
        def _():
            halo_copy(2, chunk, (up, left)).start()

    for load in loads:
        load.wait()

    for index in range(2):
        tab[2 * index], tab[2 * index + 1] = halves(made[index])
        perm[index] = made[2 + index].astype(BF16)

    def prepare(slot, carry):
        oy, ox = offs[0, 0, 0, slot], offs[0, 0, 1, slot]
        for part in range(2):
            plane = pltpu.roll(probe_v[part], oy, 0)
            turned[slot, part] = pltpu.roll(plane, ox, 1)
        rest = measured[0, 0, slot]
        total = None
        for _ in range(3):
            piece = rest.astype(BF16)
            rest = rest - piece.astype(F32)
            piece = dot(dot(perm[1], piece).astype(BF16), perm[0])
            total = piece if total is None else total + piece
        sorted_counts[slot] = total
        return carry

    lax.fori_loop(0, CAP, prepare, 0)
    gsum[...] = jnp.zeros_like(gsum)
    lsum[...] = jnp.zeros_like(lsum)
    grad[...] = jnp.zeros_like(grad)

    tw_re, tw_im = ltw[0, 0:1, :], ltw[1, 0:1, :]

    for chunk in range(CHUNKS):
        first_row = chunk * ROWS
        part = pl.ds(first_row, ROWS)
        for slot in range(2):
            halo_copy(slot, chunk, partner).wait_recv()

        @pl.when(jnp.logical_not(even))
        def _():
            forward_copy(chunk).start()

        halo_copy(2, chunk, partner).wait_recv()

        def enter(slot, carry):
            oy, ox = offs[0, 0, 0, slot], offs[0, 0, 1, slot]
            row_at = lax.broadcasted_iota(jnp.int32, (ROWS, PS), 0) + first_row
            lane_at = lax.broadcasted_iota(jnp.int32, (ROWS, PS), 1)
            is_own_row = row_at >= oy
            is_own_col = lane_at >= ox
            low_ok = row < rows_n - 1
            right_ok = col < cols_n - 1
            use_own = jnp.logical_and(is_own_row, is_own_col)
            use_right = jnp.logical_and(jnp.logical_and(is_own_row, ~is_own_col), right_ok)
            use_low = jnp.logical_and(jnp.logical_and(~is_own_row, is_own_col), low_ok)
            use_diag = jnp.logical_and(
                jnp.logical_and(~is_own_row, ~is_own_col), jnp.logical_and(low_ok, right_ok)
            )
            planes = []
            for p in range(2):
                value = jnp.where(use_own, own[p, part, :], 0.0)
                value = jnp.where(use_right, ext[0, p, part, :], value)
                value = jnp.where(use_low, ext[1, p, part, :], value)
                value = jnp.where(use_diag, ext[2, p, part, :], value)
                patch[slot, p, part, :] = value
                planes.append(value)
            valid = jnp.where(count[0, 0] > slot, 1.0, 0.0).astype(F32)
            shine = valid * (planes[0] * planes[0] + planes[1] * planes[1])
            shine = pltpu.roll(shine, lax.rem(PS - ox, PS), 1)
            for h in range(2):
                block = shine[:, h * HALF : (h + 1) * HALF]
                bright_twice[slot, h, part, :] = block
                bright_twice[slot, h, pl.ds(PS + first_row, ROWS), :] = block
            pr, pi = turned[slot, 0, part, :], turned[slot, 1, part, :]
            er = pr * planes[0] - pi * planes[1]
            ei = pr * planes[1] + pi * planes[0]
            ar, br, ai, bi = er[:, :HALF], er[:, HALF:], ei[:, :HALF], ei[:, HALF:]
            dr, di = ar - br, ai - bi
            sums = jnp.concatenate([ar + br, ai + bi], axis=1)
            diffs = jnp.concatenate([dr * tw_re - di * tw_im, dr * tw_im + di * tw_re], axis=1)
            at = pl.ds(pl.multiple_of(slot * ROWS, ROWS), ROWS)
            for parity, value in enumerate((sums, diffs)):
                high, low = halves(value)
                y_hi[parity, at, :] = high
                y_lo[parity, at, :] = low
            return carry

        lax.fori_loop(0, CAP, enter, 0)
        for parity in range(2):
            value = (
                dot(y_hi[parity], tab[0]) + dot(y_lo[parity], tab[0]) + dot(y_hi[parity], tab[1])
            )
            for slot in range(CAP):
                spec[slot, parity, part, :] = value[slot * ROWS : (slot + 1) * ROWS]

    def position(slot, carry):
        oy, ox = offs[0, 0, 0, slot], offs[0, 0, 1, slot]
        valid = jnp.where(count[0, 0] > slot, 1.0, 0.0).astype(F32)
        cr = jnp.concatenate([rtw[0], rtw[0]], axis=1)
        ci = jnp.concatenate([rtw[1], rtw[1]], axis=1)

        def block(where, half):
            piece = spec[slot, :, where, half * HALF : (half + 1) * HALF]
            return jnp.concatenate([piece[0], piece[1]], axis=1)

        top, bottom = pl.ds(0, HALF), pl.ds(HALF, HALF)
        ar, ai, br, bi = block(top, 0), block(top, 1), block(bottom, 0), block(bottom, 1)
        dr, di = ar - br, ai - bi
        sums = jnp.concatenate([ar + br, ai + bi], axis=0)
        diffs = jnp.concatenate([dr * cr - di * ci, dr * ci + di * cr], axis=0)
        backs = []
        for parity, value in enumerate((sums, diffs)):
            high, low = halves(value)
            wave = dot(tab[2], high) + dot(tab[2], low) + dot(tab[3], high)
            wr, wi = wave[:HALF], wave[HALF:]
            model = wr * wr + wi * wi + 0.5
            guess = pl.reciprocal(model, approx=True)
            guess = guess * (2.0 - model * guess)
            seen = sorted_counts[slot, parity * HALF : (parity + 1) * HALF, :]
            weight = valid - (valid * seen) * guess
            weighted = jnp.concatenate([weight * wr, weight * wi], axis=0)
            high, low = halves(weighted)
            backs.append(dot(tab[0], high) + dot(tab[0], low) + dot(tab[1], high))
        er, ei = backs[0][:HALF], backs[0][HALF:]
        dr, di = backs[1][:HALF], backs[1][HALF:]
        fr, fi = dr * cr + di * ci, di * cr - dr * ci
        vr = jnp.concatenate([er + fr, er - fr], axis=0)
        vi = jnp.concatenate([ei + fi, ei - fi], axis=0)
        ends = []
        for parity in range(2):
            lanes = slice(parity * HALF, (parity + 1) * HALF)
            high, low = halves(jnp.concatenate([vr[:, lanes], vi[:, lanes]], axis=1))
            ends.append(dot(high, tab[2]) + dot(low, tab[2]) + dot(high, tab[3]))
        er, ei = ends[0][:, :HALF], ends[0][:, HALF:]
        dr, di = ends[1][:, :HALF], ends[1][:, HALF:]
        fr, fi = dr * tw_re + di * tw_im, di * tw_re - dr * tw_im
        chi_r = jnp.concatenate([er + fr, er - fr], axis=1)
        chi_i = jnp.concatenate([ei + fi, ei - fi], axis=1)

        pr, pi = patch[slot, 0], patch[slot, 1]
        back_x = lax.rem(PS - ox, PS)
        for p, value in enumerate((pr * chi_r + pi * chi_i, pr * chi_i - pi * chi_r)):
            value = pltpu.roll(value, back_x, 1)
            for h in range(2):
                block = value[:, h * HALF : (h + 1) * HALF]
                twice[2 * p + h, :PS, :] = block
                twice[2 * p + h, PS:, :] = block
                gsum[2 * p + h] += twice[2 * p + h, pl.ds(oy, PS), :]
        spec[slot, 0] = chi_r
        spec[slot, 1] = chi_i
        return carry

    mine = pl.ds(pl.multiple_of(core * HALF, HALF), HALF)
    other = pl.ds(pl.multiple_of((1 - core) * HALF, HALF), HALF)
    mine8 = pl.ds(pl.multiple_of(rank * 8, 8), 8)
    place = pl.ds(pl.multiple_of(core * HALF + rank * 8, 8), 8)

    def remote(src, dst, send, recv, target):
        return pltpu.make_async_remote_copy(
            src_ref=src, dst_ref=dst, send_sem=send, recv_sem=recv,
            device_id=target, device_id_type=MESH,
        )

    class Sum:
        def __init__(self, full, core_in, plane_in, near_in, far_in, sems, which):
            self.full, self.core_in, self.plane_in = full, core_in, plane_in
            self.near_in, self.far_in = near_in, far_in
            (self.core_s, self.core_r, self.plane_s, self.plane_r,
             self.near_s, self.near_r, self.far_s, self.far_r) = sems
            self.which = which

        def core_copy(self):
            return remote(
                self.full.at[:, other, :], self.core_in,
                self.core_s.at[self.which], self.core_r.at[self.which], partner,
            )

        def plane_copy(self, step):
            target = lax.rem(rank + step, PLANE)
            rows8 = pl.ds(pl.multiple_of(target * 8, 8), 8)
            return remote(
                self.core_in.at[:, rows8, :], self.plane_in.at[step],
                self.plane_s.at[self.which, step], self.plane_r.at[self.which, step], on_plane(target),
            )

        def near_copy(self, step):
            return remote(
                self.near_in.at[member], self.near_in.at[member],
                self.near_s.at[self.which, step], self.near_r.at[self.which, step], at_depth(near(step)),
            )

        def near_arrival(self, step):
            at = lax.rem(member + NEAR - step, NEAR)
            return remote(
                self.near_in.at[at], self.near_in.at[at],
                self.near_s.at[self.which, step], self.near_r.at[self.which, step], partner,
            )

        def far_copy(self, step):
            return remote(
                self.far_in.at[group], self.far_in.at[group],
                self.far_s.at[self.which, step], self.far_r.at[self.which, step], at_depth(far(step)),
            )

        def far_arrival(self, step):
            at = lax.rem(group + NEAR - step, NEAR)
            return remote(
                self.far_in.at[at], self.far_in.at[at],
                self.far_s.at[self.which, step], self.far_r.at[self.which, step], partner,
            )

        def start(self):
            self.core_copy().start()

        def over_plane(self):
            self.core_copy().wait_recv()
            self.core_in[...] = self.core_in[...] + self.full[:, mine, :]
            for step in range(1, PLANE):
                self.plane_copy(step).start()

        def over_near(self):
            total = self.core_in[:, mine8, :]
            for step in range(1, PLANE):
                self.plane_copy(step).wait_recv()
                total = total + self.plane_in[step]
            self.near_in[member] = total
            for step in range(1, NEAR):
                self.near_copy(step).start()

        def over_far(self):
            for step in range(1, NEAR):
                self.near_arrival(step).wait_recv()
            self.far_in[group] = (self.near_in[0] + self.near_in[1]) + (self.near_in[2] + self.near_in[3])
            for step in range(1, NEAR):
                self.far_copy(step).start()

        def result(self):
            for step in range(1, NEAR):
                self.far_arrival(step).wait_recv()
            return (self.far_in[0] + self.far_in[1]) + (self.far_in[2] + self.far_in[3])

        def wait_sent(self):
            self.core_copy().wait_send()
            for step in range(1, PLANE):
                self.plane_copy(step).wait_send()
            for step in range(1, NEAR):
                self.near_copy(step).wait_send()
                self.far_copy(step).wait_send()

    sums = (core_send, core_recv, plane_send, plane_recv, near_send, near_recv, far_send, far_recv)
    light = Sum(lsum, core_light, plane_light, near_light, far_light, sums, 1)
    terms = Sum(gsum, core_in, plane_in, near_in, far_in, sums, 0)

    def brighten(slot, carry):
        oy = offs[0, 0, 0, slot]
        for h in range(2):
            lsum[h] += bright_twice[slot, h, pl.ds(oy, PS), :]
        return carry

    lax.fori_loop(0, CAP, brighten, 0)
    light.start()

    def step_of(slot, carry):
        position(2 * slot, carry)
        position(2 * slot + 1, carry)

        @pl.when(slot == 0)
        def _():
            light.over_plane()

        return carry

    lax.fori_loop(0, CAP // 2, step_of, 0)
    terms.start()

    def place_out(slot, carry):
        oy, ox = offs[0, 0, 0, slot], offs[0, 0, 1, slot]
        chi_r, chi_i = spec[slot, 0], spec[slot, 1]
        qr, qi = turned[slot, 0], turned[slot, 1]
        is_own_row = lax.broadcasted_iota(jnp.int32, (PS, PS), 0) >= oy
        is_own_col = lax.broadcasted_iota(jnp.int32, (PS, PS), 1) >= ox
        for p, value in enumerate((qr * chi_r + qi * chi_i, qr * chi_i - qi * chi_r)):
            here = jnp.where(is_own_col, value, 0.0)
            there = value - here
            here_own = jnp.where(is_own_row, here, 0.0)
            there_own = jnp.where(is_own_row, there, 0.0)
            grad[0, p] += here_own
            grad[1, p] += there_own
            grad[2, p] += here - here_own
            grad[3, p] += there - there_own
        return carry

    lax.fori_loop(0, CAP, place_out, 0)

    share_copy = remote(grad.at[3], shared, out_send.at[3, 0], out_recv.at[3, 0], partner)
    low_copy = remote(grad.at[2], from_out.at[1], out_send.at[1, 0], out_recv.at[1, 0], (down, col))

    def out_copy(tile, slot, piece, target):
        part = pl.ds(piece * ROWS, ROWS)
        return remote(
            grad.at[tile, :, part, :], from_out.at[slot, :, part, :],
            out_send.at[slot, piece], out_recv.at[slot, piece], target,
        )

    def right_copy(piece):
        return out_copy(1, 0, piece, (row, right))

    def diag_copy(piece):
        return out_copy(3, 2, piece, (down, right))

    inner = x_hi == 0

    def leave(who, right_pieces, diag_pieces):
        @pl.when(who)
        def _():
            for piece in diag_pieces:
                diag_copy(piece).start()
            for piece in right_pieces:
                right_copy(piece).start()

    outer_even = jnp.logical_and(jnp.logical_not(inner), even)
    outer_odd = jnp.logical_and(jnp.logical_not(inner), jnp.logical_not(even))
    inner_even = jnp.logical_and(inner, even)
    inner_odd = jnp.logical_and(inner, jnp.logical_not(even))

    @pl.when(even)
    def _():
        share_copy.start()

    leave(outer_even, (0, 1), ())
    leave(outer_odd, (), (0, 1))
    terms.over_plane()
    light.over_near()
    low_copy.start()

    @pl.when(jnp.logical_not(even))
    def _():
        share_copy.wait_recv()
        grad[1] = grad[1] + shared[...]

    leave(inner_even, range(4), ())
    leave(inner_odd, range(4), range(4))
    terms.over_near()
    light.over_far()
    leave(outer_even, (2,), ())
    leave(outer_odd, (), (2, 3))
    terms.over_far()
    leave(outer_even, (3,), ())
    leave(outer_odd, range(4), ())
    bright = light.result()
    scale = lax.rsqrt(bright + 1.0)
    total = terms.result()
    final[0, place, :] = total[0] * scale[0]
    final[1, place, :] = total[1] * scale[1]
    final[2, place, :] = total[2] * scale[0]
    final[3, place, :] = total[3] * scale[1]

    def gather_copy(step):
        return remote(
            final.at[:, place, :], final.at[:, place, :],
            gather_send.at[step], gather_recv.at[step], on_plane(lax.rem(rank + step, PLANE)),
        )

    def gather_arrival(step):
        source = lax.rem(rank + PLANE - step, PLANE)
        at = pl.ds(pl.multiple_of(core * HALF + source * 8, 8), 8)
        return remote(
            final.at[:, at, :], final.at[:, at, :],
            gather_send.at[step], gather_recv.at[step], partner,
        )

    def store_probe(where, first):
        return [
            pltpu.make_async_copy(
                final.at[block, where, :],
                out_probe.at[block // 2, where, (block % 2) * HALF : (block % 2 + 1) * HALF],
                store_sem.at[first + block],
            )
            for block in range(4)
        ]

    for step in range(1, PLANE):
        gather_copy(step).start()
    for step in range(1, PLANE):
        gather_arrival(step).wait_recv()
    last_copy = remote(final.at[:, mine, :], final.at[:, mine, :], last_send, last_recv, partner)
    last_arrival = remote(final.at[:, other, :], final.at[:, other, :], last_send, last_recv, partner)
    last_copy.start()
    stores = store_probe(mine, 0)
    for store in stores:
        store.start()

    low_copy.wait_recv()
    for piece in range(4):
        right_copy(piece).wait_recv()
    above = jnp.where(row > 0, 1.0, 0.0).astype(F32)
    before = jnp.where(col > 0, 1.0, 0.0).astype(F32)
    own[...] = grad[0] + before * from_out[0] + above * from_out[1]

    @pl.when(even)
    def _():
        for piece in range(4):
            diag_copy(piece).wait_recv()
        own[...] = own[...] + (above * before) * from_out[2]

    store_tile = pltpu.make_async_copy(own, out_obj, store_sem.at[8])
    store_tile.start()
    last_arrival.wait_recv()
    rest = store_probe(other, 4)
    for store in rest:
        store.start()

    for chunk in range(CHUNKS):
        halo_copy(0, chunk, partner).wait_send()
        halo_copy(1, chunk, partner).wait_send()

        @pl.when(even)
        def _():
            halo_copy(2, chunk, partner).wait_send()

        @pl.when(jnp.logical_not(even))
        def _():
            forward_copy(chunk).wait_send()

    light.wait_sent()
    terms.wait_sent()
    low_copy.wait_send()
    for piece in range(4):
        right_copy(piece).wait_send()

    @pl.when(even)
    def _():
        share_copy.wait_send()

    @pl.when(jnp.logical_not(even))
    def _():
        for piece in range(4):
            diag_copy(piece).wait_send()

    for step in range(1, PLANE):
        gather_copy(step).wait_send()
    last_copy.wait_send()
    for store in stores + rest:
        store.wait()
    store_tile.wait()


def finish(tile, probe, out_tile, out_probe, tile_v, probe_v, in_sem, out_sem):
    work = []
    for piece in range(4):
        part = pl.ds(piece * ROWS, ROWS)
        for index, (src, held, dst) in enumerate(
            ((tile, tile_v, out_tile), (probe, probe_v, out_probe))
        ):
            load = pltpu.make_async_copy(src.at[:, part, :], held.at[:, part, :], in_sem.at[index, piece])
            load.start()
            work.append((load, held.at[:, part, :], dst.at[:, part, :], out_sem.at[index, piece]))
    stores = []
    for load, src, dst, sem in work:
        load.wait()
        store = pltpu.make_async_copy(src, dst, sem)
        store.start()
        stores.append(store)
    for store in stores:
        store.wait()


def on_device(rows_n, cols_n, object_field, probe, counts_measured, offsets, slot_count):
    tables, lane_tw, row_tw = constants()
    any_spec = pl.BlockSpec(memory_space=pltpu.HBM)
    smem_spec = pl.BlockSpec(memory_space=pltpu.SMEM)
    tile = (2, PS, PS)
    dma = pltpu.SemaphoreType.DMA
    shapes = (jax.ShapeDtypeStruct(tile, F32), jax.ShapeDtypeStruct(tile, F32))
    results = pl.pallas_call(
        functools.partial(kernel, rows_n, cols_n),
        out_shape=(jax.ShapeDtypeStruct(tile, F32), jax.ShapeDtypeStruct(tile, F32)),
        in_specs=[any_spec, any_spec, any_spec, smem_spec, smem_spec] + [any_spec] * 3,
        out_specs=(any_spec, any_spec),
        scratch_shapes=[
            pltpu.VMEM(tile, F32),
            pltpu.VMEM((3,) + tile, F32),
            pltpu.VMEM((CAP,) + tile, F32),
            pltpu.VMEM((CAP,) + tile, F32),
            pltpu.VMEM((1, 1, CAP, PS, PS), F32),
            pltpu.VMEM((CAP, PS, PS), F32),
            pltpu.VMEM(tile, F32),
            pltpu.VMEM((4, PS, PS), F32),
            pltpu.VMEM((4, PS, PS), BF16),
            pltpu.VMEM((2, 8, HALF), F32),
            pltpu.VMEM((2, HALF, HALF), F32),
            pltpu.VMEM((2, PS, PS), BF16),
            pltpu.VMEM((2, CAP * ROWS, PS), BF16),
            pltpu.VMEM((2, CAP * ROWS, PS), BF16),
            pltpu.VMEM((CAP, 2, PS, PS), F32),
            pltpu.VMEM((4, 2 * PS, HALF), F32),
            pltpu.VMEM((CAP, 2, 2 * PS, HALF), F32),
            pltpu.VMEM((4,) + tile, F32),
            pltpu.VMEM((4, PS, HALF), F32),
            pltpu.VMEM((2, PS, HALF), F32),
            pltpu.VMEM((3,) + tile, F32),
            pltpu.VMEM(tile, F32),
            pltpu.VMEM((4, PS, HALF), F32),
            pltpu.VMEM((4, HALF, HALF), F32),
            pltpu.VMEM((PLANE, 4, 8, HALF), F32),
            pltpu.VMEM((NEAR, 4, 8, HALF), F32),
            pltpu.VMEM((NEAR, 4, 8, HALF), F32),
            pltpu.VMEM((2, HALF, HALF), F32),
            pltpu.VMEM((PLANE, 2, 8, HALF), F32),
            pltpu.VMEM((NEAR, 2, 8, HALF), F32),
            pltpu.VMEM((NEAR, 2, 8, HALF), F32),
            dma((6,)),
            dma((3, CHUNKS)),
            dma((3, CHUNKS)),
            dma((CHUNKS,)),
            dma((4, 4)),
            dma((4, 4)),
            dma((2,)),
            dma((2,)),
            dma((2, PLANE)),
            dma((2, PLANE)),
            dma((2, NEAR)),
            dma((2, NEAR)),
            dma((2, NEAR)),
            dma((2, NEAR)),
            dma((PLANE,)),
            dma((PLANE,)),
            dma,
            dma,
            dma((9,)),
        ],
        compiler_params=pltpu.CompilerParams(
            collective_id=0, has_side_effects=True, vmem_limit_bytes=60 << 20
        ),
        name="ptychography",
    )(
        object_field, probe, counts_measured, jnp.swapaxes(offsets, 2, 3), slot_count,
        jnp.asarray(tables), jnp.asarray(lane_tw), jnp.asarray(row_tw),
    )
    return pl.pallas_call(
        finish,
        out_shape=shapes,
        in_specs=[any_spec, any_spec],
        out_specs=(any_spec, any_spec),
        scratch_shapes=[
            pltpu.VMEM(tile, F32),
            pltpu.VMEM(tile, F32),
            dma((2, 4)),
            dma((2, 4)),
        ],
        compiler_params=pltpu.CompilerParams(vmem_limit_bytes=60 << 20),
        name="finish",
    )(*results)


def solution(mesh):
    rows_n, cols_n = mesh.shape["row"], mesh.shape["col"]
    return jax.shard_map(
        functools.partial(on_device, rows_n, cols_n),
        mesh=mesh,
        in_specs=(
            P(None, "row", "col"),
            P(),
            P("row", "col", None, None, None),
            P("row", "col", None, None),
            P("row", "col"),
        ),
        out_specs=(P(None, "row", "col"), P()),
        check_vma=False,
    )
```

```python
import functools
import math

import jax
import jax.numpy as jnp
import numpy as np
from jax import lax
from jax.experimental import pallas as pl
from jax.experimental.pallas import tpu as pltpu
from jax.sharding import PartitionSpec as P

MESH = pl.DeviceIdType.MESH
PS = 256
HALF = 128
CAP = 4
CHUNKS = 4
ROWS = PS // CHUNKS
PLANE = 16
NEAR = 4
F32 = jnp.float32
BF16 = jnp.bfloat16


def constants():
    n = np.arange(HALF)
    angle = 2.0 * math.pi * ((n[:, None] * n[None, :]) % HALF) / HALF
    cos, sin = np.cos(angle) / 16.0, np.sin(angle) / 16.0
    matrix = np.block([[cos, -sin], [sin, cos]])
    tables = np.stack([matrix, matrix.T]).astype(np.float32)
    turn = 2.0 * math.pi * n / PS
    tw = np.stack([np.cos(turn), -np.sin(turn)]).astype(np.float32)
    lane_tw = np.broadcast_to(tw[:, None, :], (2, 8, HALF)).copy()
    row_tw = np.broadcast_to(tw[:, :, None], (2, HALF, HALF)).copy()
    order = np.zeros((PS, PS), np.float32)
    lane = np.arange(PS)
    order[lane, (lane % 2) * HALF + lane // 2] = 1.0
    orders = np.stack([order, order.T])
    return np.concatenate([tables, orders]), lane_tw, row_tw


def dot(left, right):
    return jnp.dot(left, right, preferred_element_type=F32)


def halves(x):
    high = x.astype(BF16)
    return high, (x - high.astype(F32)).astype(BF16)


def kernel(
    rows_n,
    cols_n,
    obj, probe, counts, offs, count, tables, lane_tw, row_tw,
    out_obj, out_probe,
    own, ext, patch, turned, measured, sorted_counts, probe_v, made, tab, ltw, rtw, perm,
    y_hi, y_lo, spec, twice, bright_twice, grad, gsum, lsum, from_out, shared, final,
    core_in, plane_in, near_in, far_in, core_light, plane_light, near_light, far_light,
    load_sem, in_send, in_recv, fwd_send, out_send, out_recv,
    core_send, core_recv, plane_send, plane_recv, near_send, near_recv, far_send, far_recv,
    gather_send, gather_recv, last_send, last_recv, store_sem, hello,
):
    row, col = lax.axis_index("row"), lax.axis_index("col")
    core = lax.rem(row, 2)
    x_lo = lax.rem(row // 2, 2)
    y = row // 4
    z = col // 2
    x_hi = lax.rem(col, 2)
    depth = cols_n // 2
    rank = y * 4 + x_hi * 2 + x_lo

    def on_plane(other):
        return ((other // 4) * 4 + lax.rem(other, 2) * 2 + core, z * 2 + lax.rem(other // 2, 2))

    def at_depth(other):
        return (row, other * 2 + x_hi)

    group, member = z // NEAR, lax.rem(z, NEAR)

    def near(step):
        return group * NEAR + lax.rem(member + step, NEAR)

    def far(step):
        return lax.rem(group + step, NEAR) * NEAR + member

    up, down = lax.rem(row + rows_n - 1, rows_n), lax.rem(row + 1, rows_n)
    left, right = lax.rem(col + cols_n - 1, cols_n), lax.rem(col + 1, cols_n)
    partner = (row + 1 - 2 * core, col)
    even = core == 0

    barrier = pltpu.get_barrier_semaphore()
    known = [(row, left), (row, right), (up, col), (down, col)]
    for other in known:
        pl.semaphore_signal(barrier, inc=1, device_id=other, device_id_type=MESH)

    @pl.when(even)
    def _():
        pl.semaphore_signal(barrier, inc=1, device_id=(up, left), device_id_type=MESH)

    @pl.when(jnp.logical_not(even))
    def _():
        pl.semaphore_signal(barrier, inc=1, device_id=(down, right), device_id_type=MESH)

    for step in range(1, PLANE):
        pl.semaphore_signal(
            barrier, inc=1, device_id=on_plane(lax.rem(rank + step, PLANE)), device_id_type=MESH
        )
    for step in range(1, NEAR):
        pl.semaphore_signal(barrier, inc=1, device_id=at_depth(near(step)), device_id_type=MESH)
    first, last = member == 0, member == NEAR - 1
    before_z, after_z = at_depth(lax.rem(z + depth - 1, depth)), at_depth(lax.rem(z + 1, depth))

    @pl.when(first)
    def _():
        pl.semaphore_signal(barrier, inc=1, device_id=before_z, device_id_type=MESH)

    @pl.when(last)
    def _():
        pl.semaphore_signal(barrier, inc=1, device_id=after_z, device_id_type=MESH)

    edge = 1 - jnp.minimum(member * (NEAR - 1 - member), 1)

    loads = []
    for index, (src, dst) in enumerate(
        [
            (obj, own), (probe, probe_v), (counts, measured), (tables, made),
            (lane_tw, ltw), (row_tw, rtw),
        ]
    ):
        load = pltpu.make_async_copy(src, dst, load_sem.at[index])
        load.start()
        loads.append(load)

    pl.semaphore_wait(barrier, 5 + PLANE - 1 + NEAR - 1 + edge)

    def halo_copy(slot, chunk, target):
        part = pl.ds(chunk * ROWS, ROWS)
        return pltpu.make_async_remote_copy(
            src_ref=obj.at[:, part, :],
            dst_ref=ext.at[slot, :, part, :],
            send_sem=in_send.at[slot, chunk],
            recv_sem=in_recv.at[slot, chunk],
            device_id=target,
            device_id_type=MESH,
        )

    def forward_copy(chunk):
        part = pl.ds(chunk * ROWS, ROWS)
        return pltpu.make_async_remote_copy(
            src_ref=ext.at[0, :, part, :],
            dst_ref=ext.at[2, :, part, :],
            send_sem=fwd_send.at[chunk],
            recv_sem=in_recv.at[2, chunk],
            device_id=partner,
            device_id_type=MESH,
        )

    for chunk in range(CHUNKS):
        halo_copy(0, chunk, (row, left)).start()
        halo_copy(1, chunk, (up, col)).start()

        @pl.when(even)
        def _():
            halo_copy(2, chunk, (up, left)).start()

    @pl.when(first)
    def _():
        pl.semaphore_signal(hello.at[0], inc=1, device_id=before_z, device_id_type=MESH)

    @pl.when(last)
    def _():
        pl.semaphore_signal(hello.at[1], inc=1, device_id=after_z, device_id_type=MESH)

    for load in loads:
        load.wait()

    for index in range(2):
        tab[2 * index], tab[2 * index + 1] = halves(made[index])
        perm[index] = made[2 + index].astype(BF16)

    def prepare(slot, carry):
        oy, ox = offs[0, 0, 0, slot], offs[0, 0, 1, slot]
        for part in range(2):
            plane = pltpu.roll(probe_v[part], oy, 0)
            turned[slot, part] = pltpu.roll(plane, ox, 1)
        rest = measured[0, 0, slot]
        total = None
        for _ in range(3):
            piece = rest.astype(BF16)
            rest = rest - piece.astype(F32)
            piece = dot(dot(perm[1], piece).astype(BF16), perm[0])
            total = piece if total is None else total + piece
        sorted_counts[slot] = total
        return carry

    lax.fori_loop(0, CAP, prepare, 0)
    gsum[...] = jnp.zeros_like(gsum)
    lsum[...] = jnp.zeros_like(lsum)
    grad[...] = jnp.zeros_like(grad)

    tw_re, tw_im = ltw[0, 0:1, :], ltw[1, 0:1, :]

    @pl.when(last)
    def _():
        pl.semaphore_wait(hello.at[0], 1)
        for step in range(1, NEAR):
            pl.semaphore_signal(hello.at[2], inc=1, device_id=at_depth(near(step)), device_id_type=MESH)

    @pl.when(first)
    def _():
        pl.semaphore_wait(hello.at[1], 1)
        for step in range(1, NEAR):
            pl.semaphore_signal(hello.at[3], inc=1, device_id=at_depth(near(step)), device_id_type=MESH)

    @pl.when(jnp.logical_not(last))
    def _():
        pl.semaphore_wait(hello.at[2], 1)

    @pl.when(jnp.logical_not(first))
    def _():
        pl.semaphore_wait(hello.at[3], 1)

    pl.semaphore_signal(hello.at[4], inc=1, device_id=at_depth(far(NEAR - 1)), device_id_type=MESH)

    for chunk in range(CHUNKS):
        first_row = chunk * ROWS
        part = pl.ds(first_row, ROWS)
        for slot in range(2):
            halo_copy(slot, chunk, partner).wait_recv()

        @pl.when(jnp.logical_not(even))
        def _():
            forward_copy(chunk).start()

        halo_copy(2, chunk, partner).wait_recv()

        def enter(slot, carry):
            oy, ox = offs[0, 0, 0, slot], offs[0, 0, 1, slot]
            row_at = lax.broadcasted_iota(jnp.int32, (ROWS, PS), 0) + first_row
            lane_at = lax.broadcasted_iota(jnp.int32, (ROWS, PS), 1)
            is_own_row = row_at >= oy
            is_own_col = lane_at >= ox
            low_ok = row < rows_n - 1
            right_ok = col < cols_n - 1
            use_own = jnp.logical_and(is_own_row, is_own_col)
            use_right = jnp.logical_and(jnp.logical_and(is_own_row, ~is_own_col), right_ok)
            use_low = jnp.logical_and(jnp.logical_and(~is_own_row, is_own_col), low_ok)
            use_diag = jnp.logical_and(
                jnp.logical_and(~is_own_row, ~is_own_col), jnp.logical_and(low_ok, right_ok)
            )
            planes = []
            for p in range(2):
                value = jnp.where(use_own, own[p, part, :], 0.0)
                value = jnp.where(use_right, ext[0, p, part, :], value)
                value = jnp.where(use_low, ext[1, p, part, :], value)
                value = jnp.where(use_diag, ext[2, p, part, :], value)
                patch[slot, p, part, :] = value
                planes.append(value)
            valid = jnp.where(count[0, 0] > slot, 1.0, 0.0).astype(F32)
            shine = valid * (planes[0] * planes[0] + planes[1] * planes[1])
            shine = pltpu.roll(shine, lax.rem(PS - ox, PS), 1)
            for h in range(2):
                block = shine[:, h * HALF : (h + 1) * HALF]
                bright_twice[slot, h, part, :] = block
                bright_twice[slot, h, pl.ds(PS + first_row, ROWS), :] = block
            pr, pi = turned[slot, 0, part, :], turned[slot, 1, part, :]
            er = pr * planes[0] - pi * planes[1]
            ei = pr * planes[1] + pi * planes[0]
            ar, br, ai, bi = er[:, :HALF], er[:, HALF:], ei[:, :HALF], ei[:, HALF:]
            dr, di = ar - br, ai - bi
            sums = jnp.concatenate([ar + br, ai + bi], axis=1)
            diffs = jnp.concatenate([dr * tw_re - di * tw_im, dr * tw_im + di * tw_re], axis=1)
            at = pl.ds(pl.multiple_of(slot * ROWS, ROWS), ROWS)
            for parity, value in enumerate((sums, diffs)):
                high, low = halves(value)
                y_hi[parity, at, :] = high
                y_lo[parity, at, :] = low
            return carry

        lax.fori_loop(0, CAP, enter, 0)
        for parity in range(2):
            value = (
                dot(y_hi[parity], tab[0]) + dot(y_lo[parity], tab[0]) + dot(y_hi[parity], tab[1])
            )
            for slot in range(CAP):
                spec[slot, parity, part, :] = value[slot * ROWS : (slot + 1) * ROWS]

    def position(slot, carry):
        oy, ox = offs[0, 0, 0, slot], offs[0, 0, 1, slot]
        valid = jnp.where(count[0, 0] > slot, 1.0, 0.0).astype(F32)
        cr = jnp.concatenate([rtw[0], rtw[0]], axis=1)
        ci = jnp.concatenate([rtw[1], rtw[1]], axis=1)

        def block(where, half):
            piece = spec[slot, :, where, half * HALF : (half + 1) * HALF]
            return jnp.concatenate([piece[0], piece[1]], axis=1)

        top, bottom = pl.ds(0, HALF), pl.ds(HALF, HALF)
        ar, ai, br, bi = block(top, 0), block(top, 1), block(bottom, 0), block(bottom, 1)
        dr, di = ar - br, ai - bi
        sums = jnp.concatenate([ar + br, ai + bi], axis=0)
        diffs = jnp.concatenate([dr * cr - di * ci, dr * ci + di * cr], axis=0)
        backs = []
        for parity, value in enumerate((sums, diffs)):
            high, low = halves(value)
            wave = dot(tab[2], high) + dot(tab[2], low) + dot(tab[3], high)
            wr, wi = wave[:HALF], wave[HALF:]
            model = wr * wr + wi * wi + 0.5
            guess = pl.reciprocal(model, approx=True)
            guess = guess * (2.0 - model * guess)
            seen = sorted_counts[slot, parity * HALF : (parity + 1) * HALF, :]
            weight = valid - (valid * seen) * guess
            weighted = jnp.concatenate([weight * wr, weight * wi], axis=0)
            high, low = halves(weighted)
            backs.append(dot(tab[0], high) + dot(tab[0], low) + dot(tab[1], high))
        er, ei = backs[0][:HALF], backs[0][HALF:]
        dr, di = backs[1][:HALF], backs[1][HALF:]
        fr, fi = dr * cr + di * ci, di * cr - dr * ci
        vr = jnp.concatenate([er + fr, er - fr], axis=0)
        vi = jnp.concatenate([ei + fi, ei - fi], axis=0)
        ends = []
        for parity in range(2):
            lanes = slice(parity * HALF, (parity + 1) * HALF)
            high, low = halves(jnp.concatenate([vr[:, lanes], vi[:, lanes]], axis=1))
            ends.append(dot(high, tab[2]) + dot(low, tab[2]) + dot(high, tab[3]))
        er, ei = ends[0][:, :HALF], ends[0][:, HALF:]
        dr, di = ends[1][:, :HALF], ends[1][:, HALF:]
        fr, fi = dr * tw_re + di * tw_im, di * tw_re - dr * tw_im
        chi_r = jnp.concatenate([er + fr, er - fr], axis=1)
        chi_i = jnp.concatenate([ei + fi, ei - fi], axis=1)

        pr, pi = patch[slot, 0], patch[slot, 1]
        back_x = lax.rem(PS - ox, PS)
        for p, value in enumerate((pr * chi_r + pi * chi_i, pr * chi_i - pi * chi_r)):
            value = pltpu.roll(value, back_x, 1)
            for h in range(2):
                block = value[:, h * HALF : (h + 1) * HALF]
                twice[2 * p + h, :PS, :] = block
                twice[2 * p + h, PS:, :] = block
                gsum[2 * p + h] += twice[2 * p + h, pl.ds(oy, PS), :]
        spec[slot, 0] = chi_r
        spec[slot, 1] = chi_i
        return carry

    mine = pl.ds(pl.multiple_of(core * HALF, HALF), HALF)
    other = pl.ds(pl.multiple_of((1 - core) * HALF, HALF), HALF)
    mine8 = pl.ds(pl.multiple_of(rank * 8, 8), 8)
    place = pl.ds(pl.multiple_of(core * HALF + rank * 8, 8), 8)

    def remote(src, dst, send, recv, target):
        return pltpu.make_async_remote_copy(
            src_ref=src, dst_ref=dst, send_sem=send, recv_sem=recv,
            device_id=target, device_id_type=MESH,
        )

    class Sum:
        def __init__(self, full, core_in, plane_in, near_in, far_in, sems, which):
            self.full, self.core_in, self.plane_in = full, core_in, plane_in
            self.near_in, self.far_in = near_in, far_in
            (self.core_s, self.core_r, self.plane_s, self.plane_r,
             self.near_s, self.near_r, self.far_s, self.far_r) = sems
            self.which = which

        def core_copy(self):
            return remote(
                self.full.at[:, other, :], self.core_in,
                self.core_s.at[self.which], self.core_r.at[self.which], partner,
            )

        def plane_copy(self, step):
            target = lax.rem(rank + step, PLANE)
            rows8 = pl.ds(pl.multiple_of(target * 8, 8), 8)
            return remote(
                self.core_in.at[:, rows8, :], self.plane_in.at[step],
                self.plane_s.at[self.which, step], self.plane_r.at[self.which, step], on_plane(target),
            )

        def near_copy(self, step):
            return remote(
                self.near_in.at[member], self.near_in.at[member],
                self.near_s.at[self.which, step], self.near_r.at[self.which, step], at_depth(near(step)),
            )

        def near_arrival(self, step):
            at = lax.rem(member + NEAR - step, NEAR)
            return remote(
                self.near_in.at[at], self.near_in.at[at],
                self.near_s.at[self.which, step], self.near_r.at[self.which, step], partner,
            )

        def far_copy(self, step):
            return remote(
                self.far_in.at[group], self.far_in.at[group],
                self.far_s.at[self.which, step], self.far_r.at[self.which, step], at_depth(far(step)),
            )

        def far_arrival(self, step):
            at = lax.rem(group + NEAR - step, NEAR)
            return remote(
                self.far_in.at[at], self.far_in.at[at],
                self.far_s.at[self.which, step], self.far_r.at[self.which, step], partner,
            )

        def start(self):
            self.core_copy().start()

        def over_plane(self):
            self.core_copy().wait_recv()
            self.core_in[...] = self.core_in[...] + self.full[:, mine, :]
            for step in range(1, PLANE):
                self.plane_copy(step).start()

        def over_near(self):
            total = self.core_in[:, mine8, :]
            for step in range(1, PLANE):
                self.plane_copy(step).wait_recv()
                total = total + self.plane_in[step]
            self.near_in[member] = total
            for step in range(1, NEAR):
                self.near_copy(step).start()

        def over_far(self):
            for step in range(1, NEAR):
                self.near_arrival(step).wait_recv()
            self.far_in[group] = (self.near_in[0] + self.near_in[1]) + (self.near_in[2] + self.near_in[3])
            for step in range(1, NEAR):
                self.far_copy(step).start()

        def result(self):
            for step in range(1, NEAR):
                self.far_arrival(step).wait_recv()
            return (self.far_in[0] + self.far_in[1]) + (self.far_in[2] + self.far_in[3])

        def wait_sent(self):
            self.core_copy().wait_send()
            for step in range(1, PLANE):
                self.plane_copy(step).wait_send()
            for step in range(1, NEAR):
                self.near_copy(step).wait_send()
                self.far_copy(step).wait_send()

    sums = (core_send, core_recv, plane_send, plane_recv, near_send, near_recv, far_send, far_recv)
    light = Sum(lsum, core_light, plane_light, near_light, far_light, sums, 1)
    terms = Sum(gsum, core_in, plane_in, near_in, far_in, sums, 0)

    def brighten(slot, carry):
        oy = offs[0, 0, 0, slot]
        for h in range(2):
            lsum[h] += bright_twice[slot, h, pl.ds(oy, PS), :]
        return carry

    pl.semaphore_wait(hello.at[4], 1)
    lax.fori_loop(0, CAP, brighten, 0)
    light.start()

    def step_of(slot, carry):
        position(2 * slot, carry)
        position(2 * slot + 1, carry)

        @pl.when(slot == 0)
        def _():
            light.over_plane()

        return carry

    lax.fori_loop(0, CAP // 2, step_of, 0)
    terms.start()

    def place_out(slot, carry):
        oy, ox = offs[0, 0, 0, slot], offs[0, 0, 1, slot]
        chi_r, chi_i = spec[slot, 0], spec[slot, 1]
        qr, qi = turned[slot, 0], turned[slot, 1]
        is_own_row = lax.broadcasted_iota(jnp.int32, (PS, PS), 0) >= oy
        is_own_col = lax.broadcasted_iota(jnp.int32, (PS, PS), 1) >= ox
        for p, value in enumerate((qr * chi_r + qi * chi_i, qr * chi_i - qi * chi_r)):
            here = jnp.where(is_own_col, value, 0.0)
            there = value - here
            here_own = jnp.where(is_own_row, here, 0.0)
            there_own = jnp.where(is_own_row, there, 0.0)
            grad[0, p] += here_own
            grad[1, p] += there_own
            grad[2, p] += here - here_own
            grad[3, p] += there - there_own
        return carry

    lax.fori_loop(0, CAP, place_out, 0)

    share_copy = remote(grad.at[3], shared, out_send.at[3, 0], out_recv.at[3, 0], partner)
    low_copy = remote(grad.at[2], from_out.at[1], out_send.at[1, 0], out_recv.at[1, 0], (down, col))

    def out_copy(tile, slot, piece, target):
        part = pl.ds(piece * ROWS, ROWS)
        return remote(
            grad.at[tile, :, part, :], from_out.at[slot, :, part, :],
            out_send.at[slot, piece], out_recv.at[slot, piece], target,
        )

    def right_copy(piece):
        return out_copy(1, 0, piece, (row, right))

    def diag_copy(piece):
        return out_copy(3, 2, piece, (down, right))

    inner = x_hi == 0

    def leave(who, right_pieces, diag_pieces):
        @pl.when(who)
        def _():
            for piece in diag_pieces:
                diag_copy(piece).start()
            for piece in right_pieces:
                right_copy(piece).start()

    outer_even = jnp.logical_and(jnp.logical_not(inner), even)
    outer_odd = jnp.logical_and(jnp.logical_not(inner), jnp.logical_not(even))
    inner_even = jnp.logical_and(inner, even)
    inner_odd = jnp.logical_and(inner, jnp.logical_not(even))

    @pl.when(even)
    def _():
        share_copy.start()

    leave(outer_even, (0, 1), ())
    leave(outer_odd, (), (0, 1))
    terms.over_plane()
    light.over_near()
    low_copy.start()

    @pl.when(jnp.logical_not(even))
    def _():
        share_copy.wait_recv()
        grad[1] = grad[1] + shared[...]

    leave(inner_even, range(4), ())
    leave(inner_odd, range(4), range(4))
    terms.over_near()
    light.over_far()
    leave(outer_even, (2,), ())
    leave(outer_odd, (), (2, 3))
    terms.over_far()
    leave(outer_even, (3,), ())
    leave(outer_odd, range(4), ())
    bright = light.result()
    scale = lax.rsqrt(bright + 1.0)
    total = terms.result()
    final[0, place, :] = total[0] * scale[0]
    final[1, place, :] = total[1] * scale[1]
    final[2, place, :] = total[2] * scale[0]
    final[3, place, :] = total[3] * scale[1]

    def gather_copy(step):
        return remote(
            final.at[:, place, :], final.at[:, place, :],
            gather_send.at[step], gather_recv.at[step], on_plane(lax.rem(rank + step, PLANE)),
        )

    def gather_arrival(step):
        source = lax.rem(rank + PLANE - step, PLANE)
        at = pl.ds(pl.multiple_of(core * HALF + source * 8, 8), 8)
        return remote(
            final.at[:, at, :], final.at[:, at, :],
            gather_send.at[step], gather_recv.at[step], partner,
        )

    def store_probe(where, first):
        return [
            pltpu.make_async_copy(
                final.at[block, where, :],
                out_probe.at[block // 2, where, (block % 2) * HALF : (block % 2 + 1) * HALF],
                store_sem.at[first + block],
            )
            for block in range(4)
        ]

    for step in range(1, PLANE):
        gather_copy(step).start()
    for step in range(1, PLANE):
        gather_arrival(step).wait_recv()
    last_copy = remote(final.at[:, mine, :], final.at[:, mine, :], last_send, last_recv, partner)
    last_arrival = remote(final.at[:, other, :], final.at[:, other, :], last_send, last_recv, partner)
    last_copy.start()
    stores = store_probe(mine, 0)
    for store in stores:
        store.start()

    low_copy.wait_recv()
    for piece in range(4):
        right_copy(piece).wait_recv()
    above = jnp.where(row > 0, 1.0, 0.0).astype(F32)
    before = jnp.where(col > 0, 1.0, 0.0).astype(F32)
    own[...] = grad[0] + before * from_out[0] + above * from_out[1]

    @pl.when(even)
    def _():
        for piece in range(4):
            diag_copy(piece).wait_recv()
        own[...] = own[...] + (above * before) * from_out[2]

    store_tile = pltpu.make_async_copy(own, out_obj, store_sem.at[8])
    store_tile.start()
    last_arrival.wait_recv()
    rest = store_probe(other, 4)
    for store in rest:
        store.start()

    for chunk in range(CHUNKS):
        halo_copy(0, chunk, partner).wait_send()
        halo_copy(1, chunk, partner).wait_send()

        @pl.when(even)
        def _():
            halo_copy(2, chunk, partner).wait_send()

        @pl.when(jnp.logical_not(even))
        def _():
            forward_copy(chunk).wait_send()

    light.wait_sent()
    terms.wait_sent()
    low_copy.wait_send()
    for piece in range(4):
        right_copy(piece).wait_send()

    @pl.when(even)
    def _():
        share_copy.wait_send()

    @pl.when(jnp.logical_not(even))
    def _():
        for piece in range(4):
            diag_copy(piece).wait_send()

    for step in range(1, PLANE):
        gather_copy(step).wait_send()
    last_copy.wait_send()
    for store in stores + rest:
        store.wait()
    store_tile.wait()


def finish(tile, probe, out_tile, out_probe, tile_v, probe_v, in_sem, out_sem):
    work = []
    for piece in range(4):
        part = pl.ds(piece * ROWS, ROWS)
        for index, (src, held, dst) in enumerate(
            ((tile, tile_v, out_tile), (probe, probe_v, out_probe))
        ):
            load = pltpu.make_async_copy(src.at[:, part, :], held.at[:, part, :], in_sem.at[index, piece])
            load.start()
            work.append((load, held.at[:, part, :], dst.at[:, part, :], out_sem.at[index, piece]))
    stores = []
    for load, src, dst, sem in work:
        load.wait()
        store = pltpu.make_async_copy(src, dst, sem)
        store.start()
        stores.append(store)
    for store in stores:
        store.wait()


def on_device(rows_n, cols_n, object_field, probe, counts_measured, offsets, slot_count):
    tables, lane_tw, row_tw = constants()
    any_spec = pl.BlockSpec(memory_space=pltpu.HBM)
    smem_spec = pl.BlockSpec(memory_space=pltpu.SMEM)
    tile = (2, PS, PS)
    dma = pltpu.SemaphoreType.DMA
    shapes = (jax.ShapeDtypeStruct(tile, F32), jax.ShapeDtypeStruct(tile, F32))
    results = pl.pallas_call(
        functools.partial(kernel, rows_n, cols_n),
        out_shape=(jax.ShapeDtypeStruct(tile, F32), jax.ShapeDtypeStruct(tile, F32)),
        in_specs=[any_spec, any_spec, any_spec, smem_spec, smem_spec] + [any_spec] * 3,
        out_specs=(any_spec, any_spec),
        scratch_shapes=[
            pltpu.VMEM(tile, F32),
            pltpu.VMEM((3,) + tile, F32),
            pltpu.VMEM((CAP,) + tile, F32),
            pltpu.VMEM((CAP,) + tile, F32),
            pltpu.VMEM((1, 1, CAP, PS, PS), F32),
            pltpu.VMEM((CAP, PS, PS), F32),
            pltpu.VMEM(tile, F32),
            pltpu.VMEM((4, PS, PS), F32),
            pltpu.VMEM((4, PS, PS), BF16),
            pltpu.VMEM((2, 8, HALF), F32),
            pltpu.VMEM((2, HALF, HALF), F32),
            pltpu.VMEM((2, PS, PS), BF16),
            pltpu.VMEM((2, CAP * ROWS, PS), BF16),
            pltpu.VMEM((2, CAP * ROWS, PS), BF16),
            pltpu.VMEM((CAP, 2, PS, PS), F32),
            pltpu.VMEM((4, 2 * PS, HALF), F32),
            pltpu.VMEM((CAP, 2, 2 * PS, HALF), F32),
            pltpu.VMEM((4,) + tile, F32),
            pltpu.VMEM((4, PS, HALF), F32),
            pltpu.VMEM((2, PS, HALF), F32),
            pltpu.VMEM((3,) + tile, F32),
            pltpu.VMEM(tile, F32),
            pltpu.VMEM((4, PS, HALF), F32),
            pltpu.VMEM((4, HALF, HALF), F32),
            pltpu.VMEM((PLANE, 4, 8, HALF), F32),
            pltpu.VMEM((NEAR, 4, 8, HALF), F32),
            pltpu.VMEM((NEAR, 4, 8, HALF), F32),
            pltpu.VMEM((2, HALF, HALF), F32),
            pltpu.VMEM((PLANE, 2, 8, HALF), F32),
            pltpu.VMEM((NEAR, 2, 8, HALF), F32),
            pltpu.VMEM((NEAR, 2, 8, HALF), F32),
            dma((6,)),
            dma((3, CHUNKS)),
            dma((3, CHUNKS)),
            dma((CHUNKS,)),
            dma((4, 4)),
            dma((4, 4)),
            dma((2,)),
            dma((2,)),
            dma((2, PLANE)),
            dma((2, PLANE)),
            dma((2, NEAR)),
            dma((2, NEAR)),
            dma((2, NEAR)),
            dma((2, NEAR)),
            dma((PLANE,)),
            dma((PLANE,)),
            dma,
            dma,
            dma((9,)),
            pltpu.SemaphoreType.REGULAR((5,)),
        ],
        compiler_params=pltpu.CompilerParams(
            collective_id=0, has_side_effects=True, vmem_limit_bytes=60 << 20
        ),
        name="ptychography",
    )(
        object_field, probe, counts_measured, jnp.swapaxes(offsets, 2, 3), slot_count,
        jnp.asarray(tables), jnp.asarray(lane_tw), jnp.asarray(row_tw),
    )
    return pl.pallas_call(
        finish,
        out_shape=shapes,
        in_specs=[any_spec, any_spec],
        out_specs=(any_spec, any_spec),
        scratch_shapes=[
            pltpu.VMEM(tile, F32),
            pltpu.VMEM(tile, F32),
            dma((2, 4)),
            dma((2, 4)),
        ],
        compiler_params=pltpu.CompilerParams(vmem_limit_bytes=60 << 20),
        name="finish",
    )(*results)


def solution(mesh):
    rows_n, cols_n = mesh.shape["row"], mesh.shape["col"]
    return jax.shard_map(
        functools.partial(on_device, rows_n, cols_n),
        mesh=mesh,
        in_specs=(
            P(None, "row", "col"),
            P(),
            P("row", "col", None, None, None),
            P("row", "col", None, None),
            P("row", "col"),
        ),
        out_specs=(P(None, "row", "col"), P()),
        check_vma=False,
    )
```

```python
import functools
import math

import jax
import jax.numpy as jnp
import numpy as np
from jax import lax
from jax.experimental import pallas as pl
from jax.experimental.pallas import tpu as pltpu
from jax.sharding import PartitionSpec as P

MESH = pl.DeviceIdType.MESH
PS = 256
HALF = 128
CAP = 4
CHUNKS = 8
ROWS = PS // CHUNKS
PIECE = PS // 4
PLANE = 16
NEAR = 4
F32 = jnp.float32
BF16 = jnp.bfloat16


def constants():
    n = np.arange(HALF)
    angle = 2.0 * math.pi * ((n[:, None] * n[None, :]) % HALF) / HALF
    cos, sin = np.cos(angle) / 16.0, np.sin(angle) / 16.0
    matrix = np.block([[cos, -sin], [sin, cos]])
    tables = np.stack([matrix, matrix.T]).astype(np.float32)
    turn = 2.0 * math.pi * n / PS
    tw = np.stack([np.cos(turn), -np.sin(turn)]).astype(np.float32)
    lane_tw = np.broadcast_to(tw[:, None, :], (2, 8, HALF)).copy()
    row_tw = np.broadcast_to(tw[:, :, None], (2, HALF, HALF)).copy()
    order = np.zeros((PS, PS), np.float32)
    lane = np.arange(PS)
    order[lane, (lane % 2) * HALF + lane // 2] = 1.0
    orders = np.stack([order, order.T])
    return np.concatenate([tables, orders]), lane_tw, row_tw


def dot(left, right):
    return jnp.dot(left, right, preferred_element_type=F32)


def halves(x):
    high = x.astype(BF16)
    return high, (x - high.astype(F32)).astype(BF16)


def kernel(
    rows_n,
    cols_n,
    obj, probe, counts, offs, count, tables, lane_tw, row_tw,
    out_obj, out_probe,
    own, ext, patch, turned, measured, sorted_counts, probe_v, made, tab, ltw, rtw, perm,
    y_hi, y_lo, spec, twice, bright_twice, grad, gsum, lsum, from_out, shared, final,
    core_in, plane_in, near_in, far_in, core_light, plane_light, near_light, far_light,
    load_sem, in_send, in_recv, fwd_send, out_send, out_recv,
    core_send, core_recv, plane_send, plane_recv, near_send, near_recv, far_send, far_recv,
    gather_send, gather_recv, last_send, last_recv, store_sem, hello,
):
    row, col = lax.axis_index("row"), lax.axis_index("col")
    core = lax.rem(row, 2)
    x_lo = lax.rem(row // 2, 2)
    y = row // 4
    z = col // 2
    x_hi = lax.rem(col, 2)
    depth = cols_n // 2
    rank = y * 4 + x_hi * 2 + x_lo

    def on_plane(other):
        return ((other // 4) * 4 + lax.rem(other, 2) * 2 + core, z * 2 + lax.rem(other // 2, 2))

    def at_depth(other):
        return (row, other * 2 + x_hi)

    group, member = z // NEAR, lax.rem(z, NEAR)

    def near(step):
        return group * NEAR + lax.rem(member + step, NEAR)

    def far(step):
        return lax.rem(group + step, NEAR) * NEAR + member

    up, down = lax.rem(row + rows_n - 1, rows_n), lax.rem(row + 1, rows_n)
    left, right = lax.rem(col + cols_n - 1, cols_n), lax.rem(col + 1, cols_n)
    partner = (row + 1 - 2 * core, col)
    even = core == 0

    barrier = pltpu.get_barrier_semaphore()
    known = [(row, left), (row, right), (up, col), (down, col)]
    for other in known:
        pl.semaphore_signal(barrier, inc=1, device_id=other, device_id_type=MESH)

    @pl.when(even)
    def _():
        pl.semaphore_signal(barrier, inc=1, device_id=(up, left), device_id_type=MESH)

    @pl.when(jnp.logical_not(even))
    def _():
        pl.semaphore_signal(barrier, inc=1, device_id=(down, right), device_id_type=MESH)

    for step in range(1, PLANE):
        pl.semaphore_signal(
            barrier, inc=1, device_id=on_plane(lax.rem(rank + step, PLANE)), device_id_type=MESH
        )
    for step in range(1, NEAR):
        pl.semaphore_signal(barrier, inc=1, device_id=at_depth(near(step)), device_id_type=MESH)
    first, last = member == 0, member == NEAR - 1
    before_z, after_z = at_depth(lax.rem(z + depth - 1, depth)), at_depth(lax.rem(z + 1, depth))

    @pl.when(first)
    def _():
        pl.semaphore_signal(barrier, inc=1, device_id=before_z, device_id_type=MESH)

    @pl.when(last)
    def _():
        pl.semaphore_signal(barrier, inc=1, device_id=after_z, device_id_type=MESH)

    edge = 1 - jnp.minimum(member * (NEAR - 1 - member), 1)

    loads = []
    for index, (src, dst) in enumerate(
        [
            (obj, own), (probe, probe_v), (counts, measured), (tables, made),
            (lane_tw, ltw), (row_tw, rtw),
        ]
    ):
        load = pltpu.make_async_copy(src, dst, load_sem.at[index])
        load.start()
        loads.append(load)

    pl.semaphore_wait(barrier, 5 + PLANE - 1 + NEAR - 1 + edge)

    def halo_copy(slot, chunk, target):
        part = pl.ds(chunk * ROWS, ROWS)
        return pltpu.make_async_remote_copy(
            src_ref=obj.at[:, part, :],
            dst_ref=ext.at[slot, :, part, :],
            send_sem=in_send.at[slot, chunk],
            recv_sem=in_recv.at[slot, chunk],
            device_id=target,
            device_id_type=MESH,
        )

    def forward_copy(chunk):
        part = pl.ds(chunk * ROWS, ROWS)
        return pltpu.make_async_remote_copy(
            src_ref=ext.at[0, :, part, :],
            dst_ref=ext.at[2, :, part, :],
            send_sem=fwd_send.at[chunk],
            recv_sem=in_recv.at[2, chunk],
            device_id=partner,
            device_id_type=MESH,
        )

    for chunk in range(CHUNKS):
        halo_copy(0, chunk, (row, left)).start()
        halo_copy(1, chunk, (up, col)).start()

        @pl.when(even)
        def _():
            halo_copy(2, chunk, (up, left)).start()

    @pl.when(first)
    def _():
        pl.semaphore_signal(hello.at[0], inc=1, device_id=before_z, device_id_type=MESH)

    @pl.when(last)
    def _():
        pl.semaphore_signal(hello.at[1], inc=1, device_id=after_z, device_id_type=MESH)

    for load in loads:
        load.wait()

    for index in range(2):
        tab[2 * index], tab[2 * index + 1] = halves(made[index])
        perm[index] = made[2 + index].astype(BF16)

    def prepare(slot, carry):
        oy, ox = offs[0, 0, 0, slot], offs[0, 0, 1, slot]
        for part in range(2):
            plane = pltpu.roll(probe_v[part], oy, 0)
            turned[slot, part] = pltpu.roll(plane, ox, 1)
        rest = measured[0, 0, slot]
        total = None
        for _ in range(3):
            piece = rest.astype(BF16)
            rest = rest - piece.astype(F32)
            piece = dot(dot(perm[1], piece).astype(BF16), perm[0])
            total = piece if total is None else total + piece
        sorted_counts[slot] = total
        return carry

    lax.fori_loop(0, CAP, prepare, 0)
    gsum[...] = jnp.zeros_like(gsum)
    lsum[...] = jnp.zeros_like(lsum)
    grad[...] = jnp.zeros_like(grad)

    tw_re, tw_im = ltw[0, 0:1, :], ltw[1, 0:1, :]

    @pl.when(last)
    def _():
        pl.semaphore_wait(hello.at[0], 1)
        for step in range(1, NEAR):
            pl.semaphore_signal(hello.at[2], inc=1, device_id=at_depth(near(step)), device_id_type=MESH)

    @pl.when(first)
    def _():
        pl.semaphore_wait(hello.at[1], 1)
        for step in range(1, NEAR):
            pl.semaphore_signal(hello.at[3], inc=1, device_id=at_depth(near(step)), device_id_type=MESH)

    @pl.when(jnp.logical_not(last))
    def _():
        pl.semaphore_wait(hello.at[2], 1)

    @pl.when(jnp.logical_not(first))
    def _():
        pl.semaphore_wait(hello.at[3], 1)

    pl.semaphore_signal(hello.at[4], inc=1, device_id=at_depth(far(NEAR - 1)), device_id_type=MESH)

    for chunk in range(CHUNKS):
        first_row = chunk * ROWS
        part = pl.ds(first_row, ROWS)
        for slot in range(2):
            halo_copy(slot, chunk, partner).wait_recv()

        @pl.when(jnp.logical_not(even))
        def _():
            forward_copy(chunk).start()

        halo_copy(2, chunk, partner).wait_recv()

        def enter(slot, carry):
            oy, ox = offs[0, 0, 0, slot], offs[0, 0, 1, slot]
            row_at = lax.broadcasted_iota(jnp.int32, (ROWS, PS), 0) + first_row
            lane_at = lax.broadcasted_iota(jnp.int32, (ROWS, PS), 1)
            is_own_row = row_at >= oy
            is_own_col = lane_at >= ox
            low_ok = row < rows_n - 1
            right_ok = col < cols_n - 1
            use_own = jnp.logical_and(is_own_row, is_own_col)
            use_right = jnp.logical_and(jnp.logical_and(is_own_row, ~is_own_col), right_ok)
            use_low = jnp.logical_and(jnp.logical_and(~is_own_row, is_own_col), low_ok)
            use_diag = jnp.logical_and(
                jnp.logical_and(~is_own_row, ~is_own_col), jnp.logical_and(low_ok, right_ok)
            )
            planes = []
            for p in range(2):
                value = jnp.where(use_own, own[p, part, :], 0.0)
                value = jnp.where(use_right, ext[0, p, part, :], value)
                value = jnp.where(use_low, ext[1, p, part, :], value)
                value = jnp.where(use_diag, ext[2, p, part, :], value)
                patch[slot, p, part, :] = value
                planes.append(value)
            valid = jnp.where(count[0, 0] > slot, 1.0, 0.0).astype(F32)
            shine = valid * (planes[0] * planes[0] + planes[1] * planes[1])
            shine = pltpu.roll(shine, lax.rem(PS - ox, PS), 1)
            for h in range(2):
                block = shine[:, h * HALF : (h + 1) * HALF]
                bright_twice[slot, h, part, :] = block
                bright_twice[slot, h, pl.ds(PS + first_row, ROWS), :] = block
            pr, pi = turned[slot, 0, part, :], turned[slot, 1, part, :]
            er = pr * planes[0] - pi * planes[1]
            ei = pr * planes[1] + pi * planes[0]
            ar, br, ai, bi = er[:, :HALF], er[:, HALF:], ei[:, :HALF], ei[:, HALF:]
            dr, di = ar - br, ai - bi
            sums = jnp.concatenate([ar + br, ai + bi], axis=1)
            diffs = jnp.concatenate([dr * tw_re - di * tw_im, dr * tw_im + di * tw_re], axis=1)
            at = pl.ds(pl.multiple_of(slot * ROWS, ROWS), ROWS)
            for parity, value in enumerate((sums, diffs)):
                high, low = halves(value)
                y_hi[parity, at, :] = high
                y_lo[parity, at, :] = low
            return carry

        lax.fori_loop(0, CAP, enter, 0)
        for parity in range(2):
            value = (
                dot(y_hi[parity], tab[0]) + dot(y_lo[parity], tab[0]) + dot(y_hi[parity], tab[1])
            )
            for slot in range(CAP):
                spec[slot, parity, part, :] = value[slot * ROWS : (slot + 1) * ROWS]

    def position(slot, carry):
        oy, ox = offs[0, 0, 0, slot], offs[0, 0, 1, slot]
        valid = jnp.where(count[0, 0] > slot, 1.0, 0.0).astype(F32)
        cr = jnp.concatenate([rtw[0], rtw[0]], axis=1)
        ci = jnp.concatenate([rtw[1], rtw[1]], axis=1)

        def block(where, half):
            piece = spec[slot, :, where, half * HALF : (half + 1) * HALF]
            return jnp.concatenate([piece[0], piece[1]], axis=1)

        top, bottom = pl.ds(0, HALF), pl.ds(HALF, HALF)
        ar, ai, br, bi = block(top, 0), block(top, 1), block(bottom, 0), block(bottom, 1)
        dr, di = ar - br, ai - bi
        sums = jnp.concatenate([ar + br, ai + bi], axis=0)
        diffs = jnp.concatenate([dr * cr - di * ci, dr * ci + di * cr], axis=0)
        backs = []
        for parity, value in enumerate((sums, diffs)):
            high, low = halves(value)
            wave = dot(tab[2], high) + dot(tab[2], low) + dot(tab[3], high)
            wr, wi = wave[:HALF], wave[HALF:]
            model = wr * wr + wi * wi + 0.5
            guess = pl.reciprocal(model, approx=True)
            guess = guess * (2.0 - model * guess)
            seen = sorted_counts[slot, parity * HALF : (parity + 1) * HALF, :]
            weight = valid - (valid * seen) * guess
            weighted = jnp.concatenate([weight * wr, weight * wi], axis=0)
            high, low = halves(weighted)
            backs.append(dot(tab[0], high) + dot(tab[0], low) + dot(tab[1], high))
        er, ei = backs[0][:HALF], backs[0][HALF:]
        dr, di = backs[1][:HALF], backs[1][HALF:]
        fr, fi = dr * cr + di * ci, di * cr - dr * ci
        vr = jnp.concatenate([er + fr, er - fr], axis=0)
        vi = jnp.concatenate([ei + fi, ei - fi], axis=0)
        ends = []
        for parity in range(2):
            lanes = slice(parity * HALF, (parity + 1) * HALF)
            high, low = halves(jnp.concatenate([vr[:, lanes], vi[:, lanes]], axis=1))
            ends.append(dot(high, tab[2]) + dot(low, tab[2]) + dot(high, tab[3]))
        er, ei = ends[0][:, :HALF], ends[0][:, HALF:]
        dr, di = ends[1][:, :HALF], ends[1][:, HALF:]
        fr, fi = dr * tw_re + di * tw_im, di * tw_re - dr * tw_im
        chi_r = jnp.concatenate([er + fr, er - fr], axis=1)
        chi_i = jnp.concatenate([ei + fi, ei - fi], axis=1)

        pr, pi = patch[slot, 0], patch[slot, 1]
        back_x = lax.rem(PS - ox, PS)
        for p, value in enumerate((pr * chi_r + pi * chi_i, pr * chi_i - pi * chi_r)):
            value = pltpu.roll(value, back_x, 1)
            for h in range(2):
                block = value[:, h * HALF : (h + 1) * HALF]
                twice[2 * p + h, :PS, :] = block
                twice[2 * p + h, PS:, :] = block
                gsum[2 * p + h] += twice[2 * p + h, pl.ds(oy, PS), :]
        spec[slot, 0] = chi_r
        spec[slot, 1] = chi_i
        return carry

    mine = pl.ds(pl.multiple_of(core * HALF, HALF), HALF)
    other = pl.ds(pl.multiple_of((1 - core) * HALF, HALF), HALF)
    mine8 = pl.ds(pl.multiple_of(rank * 8, 8), 8)
    place = pl.ds(pl.multiple_of(core * HALF + rank * 8, 8), 8)

    def remote(src, dst, send, recv, target):
        return pltpu.make_async_remote_copy(
            src_ref=src, dst_ref=dst, send_sem=send, recv_sem=recv,
            device_id=target, device_id_type=MESH,
        )

    class Sum:
        def __init__(self, full, core_in, plane_in, near_in, far_in, sems, which):
            self.full, self.core_in, self.plane_in = full, core_in, plane_in
            self.near_in, self.far_in = near_in, far_in
            (self.core_s, self.core_r, self.plane_s, self.plane_r,
             self.near_s, self.near_r, self.far_s, self.far_r) = sems
            self.which = which

        def core_copy(self):
            return remote(
                self.full.at[:, other, :], self.core_in,
                self.core_s.at[self.which], self.core_r.at[self.which], partner,
            )

        def plane_copy(self, step):
            target = lax.rem(rank + step, PLANE)
            rows8 = pl.ds(pl.multiple_of(target * 8, 8), 8)
            return remote(
                self.core_in.at[:, rows8, :], self.plane_in.at[step],
                self.plane_s.at[self.which, step], self.plane_r.at[self.which, step], on_plane(target),
            )

        def near_copy(self, step):
            return remote(
                self.near_in.at[member], self.near_in.at[member],
                self.near_s.at[self.which, step], self.near_r.at[self.which, step], at_depth(near(step)),
            )

        def near_arrival(self, step):
            at = lax.rem(member + NEAR - step, NEAR)
            return remote(
                self.near_in.at[at], self.near_in.at[at],
                self.near_s.at[self.which, step], self.near_r.at[self.which, step], partner,
            )

        def far_copy(self, step):
            return remote(
                self.far_in.at[group], self.far_in.at[group],
                self.far_s.at[self.which, step], self.far_r.at[self.which, step], at_depth(far(step)),
            )

        def far_arrival(self, step):
            at = lax.rem(group + NEAR - step, NEAR)
            return remote(
                self.far_in.at[at], self.far_in.at[at],
                self.far_s.at[self.which, step], self.far_r.at[self.which, step], partner,
            )

        def start(self):
            self.core_copy().start()

        def over_plane(self):
            self.core_copy().wait_recv()
            self.core_in[...] = self.core_in[...] + self.full[:, mine, :]
            for step in range(1, PLANE):
                self.plane_copy(step).start()

        def over_near(self):
            total = self.core_in[:, mine8, :]
            for step in range(1, PLANE):
                self.plane_copy(step).wait_recv()
                total = total + self.plane_in[step]
            self.near_in[member] = total
            for step in range(1, NEAR):
                self.near_copy(step).start()

        def over_far(self):
            for step in range(1, NEAR):
                self.near_arrival(step).wait_recv()
            self.far_in[group] = (self.near_in[0] + self.near_in[1]) + (self.near_in[2] + self.near_in[3])
            for step in range(1, NEAR):
                self.far_copy(step).start()

        def result(self):
            for step in range(1, NEAR):
                self.far_arrival(step).wait_recv()
            return (self.far_in[0] + self.far_in[1]) + (self.far_in[2] + self.far_in[3])

        def wait_sent(self):
            self.core_copy().wait_send()
            for step in range(1, PLANE):
                self.plane_copy(step).wait_send()
            for step in range(1, NEAR):
                self.near_copy(step).wait_send()
                self.far_copy(step).wait_send()

    sums = (core_send, core_recv, plane_send, plane_recv, near_send, near_recv, far_send, far_recv)
    light = Sum(lsum, core_light, plane_light, near_light, far_light, sums, 1)
    terms = Sum(gsum, core_in, plane_in, near_in, far_in, sums, 0)

    def brighten(slot, carry):
        oy = offs[0, 0, 0, slot]
        for h in range(2):
            lsum[h] += bright_twice[slot, h, pl.ds(oy, PS), :]
        return carry

    pl.semaphore_wait(hello.at[4], 1)
    lax.fori_loop(0, CAP, brighten, 0)
    light.start()

    def step_of(slot, carry):
        position(2 * slot, carry)
        position(2 * slot + 1, carry)

        @pl.when(slot == 0)
        def _():
            light.over_plane()

        return carry

    lax.fori_loop(0, CAP // 2, step_of, 0)
    terms.start()

    def place_out(slot, carry):
        oy, ox = offs[0, 0, 0, slot], offs[0, 0, 1, slot]
        chi_r, chi_i = spec[slot, 0], spec[slot, 1]
        qr, qi = turned[slot, 0], turned[slot, 1]
        is_own_row = lax.broadcasted_iota(jnp.int32, (PS, PS), 0) >= oy
        is_own_col = lax.broadcasted_iota(jnp.int32, (PS, PS), 1) >= ox
        for p, value in enumerate((qr * chi_r + qi * chi_i, qr * chi_i - qi * chi_r)):
            here = jnp.where(is_own_col, value, 0.0)
            there = value - here
            here_own = jnp.where(is_own_row, here, 0.0)
            there_own = jnp.where(is_own_row, there, 0.0)
            grad[0, p] += here_own
            grad[1, p] += there_own
            grad[2, p] += here - here_own
            grad[3, p] += there - there_own
        return carry

    lax.fori_loop(0, CAP, place_out, 0)

    share_copy = remote(grad.at[3], shared, out_send.at[3, 0], out_recv.at[3, 0], partner)
    low_copy = remote(grad.at[2], from_out.at[1], out_send.at[1, 0], out_recv.at[1, 0], (down, col))

    def out_copy(tile, slot, piece, target):
        part = pl.ds(piece * PIECE, PIECE)
        return remote(
            grad.at[tile, :, part, :], from_out.at[slot, :, part, :],
            out_send.at[slot, piece], out_recv.at[slot, piece], target,
        )

    def right_copy(piece):
        return out_copy(1, 0, piece, (row, right))

    def diag_copy(piece):
        return out_copy(3, 2, piece, (down, right))

    inner = x_hi == 0

    def leave(who, right_pieces, diag_pieces):
        @pl.when(who)
        def _():
            for piece in diag_pieces:
                diag_copy(piece).start()
            for piece in right_pieces:
                right_copy(piece).start()

    outer_even = jnp.logical_and(jnp.logical_not(inner), even)
    outer_odd = jnp.logical_and(jnp.logical_not(inner), jnp.logical_not(even))
    inner_even = jnp.logical_and(inner, even)
    inner_odd = jnp.logical_and(inner, jnp.logical_not(even))

    @pl.when(even)
    def _():
        share_copy.start()

    leave(outer_even, (0, 1), ())
    leave(outer_odd, (), (0, 1))
    terms.over_plane()
    light.over_near()
    low_copy.start()

    @pl.when(jnp.logical_not(even))
    def _():
        share_copy.wait_recv()
        grad[1] = grad[1] + shared[...]

    leave(inner_even, range(4), ())
    leave(inner_odd, range(4), range(4))
    terms.over_near()
    light.over_far()
    leave(outer_even, (2,), ())
    leave(outer_odd, (), (2, 3))
    terms.over_far()
    leave(outer_even, (3,), ())
    leave(outer_odd, range(4), ())
    bright = light.result()
    scale = lax.rsqrt(bright + 1.0)
    total = terms.result()
    final[0, place, :] = total[0] * scale[0]
    final[1, place, :] = total[1] * scale[1]
    final[2, place, :] = total[2] * scale[0]
    final[3, place, :] = total[3] * scale[1]

    def gather_copy(step):
        return remote(
            final.at[:, place, :], final.at[:, place, :],
            gather_send.at[step], gather_recv.at[step], on_plane(lax.rem(rank + step, PLANE)),
        )

    def gather_arrival(step):
        source = lax.rem(rank + PLANE - step, PLANE)
        at = pl.ds(pl.multiple_of(core * HALF + source * 8, 8), 8)
        return remote(
            final.at[:, at, :], final.at[:, at, :],
            gather_send.at[step], gather_recv.at[step], partner,
        )

    def store_probe(where, first):
        return [
            pltpu.make_async_copy(
                final.at[block, where, :],
                out_probe.at[block // 2, where, (block % 2) * HALF : (block % 2 + 1) * HALF],
                store_sem.at[first + block],
            )
            for block in range(4)
        ]

    for step in range(1, PLANE):
        gather_copy(step).start()
    for step in range(1, PLANE):
        gather_arrival(step).wait_recv()
    last_copy = remote(final.at[:, mine, :], final.at[:, mine, :], last_send, last_recv, partner)
    last_arrival = remote(final.at[:, other, :], final.at[:, other, :], last_send, last_recv, partner)
    last_copy.start()
    stores = store_probe(mine, 0)
    for store in stores:
        store.start()

    low_copy.wait_recv()
    for piece in range(4):
        right_copy(piece).wait_recv()
    above = jnp.where(row > 0, 1.0, 0.0).astype(F32)
    before = jnp.where(col > 0, 1.0, 0.0).astype(F32)
    own[...] = grad[0] + before * from_out[0] + above * from_out[1]

    @pl.when(even)
    def _():
        for piece in range(4):
            diag_copy(piece).wait_recv()
        own[...] = own[...] + (above * before) * from_out[2]

    store_tile = pltpu.make_async_copy(own, out_obj, store_sem.at[8])
    store_tile.start()
    last_arrival.wait_recv()
    rest = store_probe(other, 4)
    for store in rest:
        store.start()

    for chunk in range(CHUNKS):
        halo_copy(0, chunk, partner).wait_send()
        halo_copy(1, chunk, partner).wait_send()

        @pl.when(even)
        def _():
            halo_copy(2, chunk, partner).wait_send()

        @pl.when(jnp.logical_not(even))
        def _():
            forward_copy(chunk).wait_send()

    light.wait_sent()
    terms.wait_sent()
    low_copy.wait_send()
    for piece in range(4):
        right_copy(piece).wait_send()

    @pl.when(even)
    def _():
        share_copy.wait_send()

    @pl.when(jnp.logical_not(even))
    def _():
        for piece in range(4):
            diag_copy(piece).wait_send()

    for step in range(1, PLANE):
        gather_copy(step).wait_send()
    last_copy.wait_send()
    for store in stores + rest:
        store.wait()
    store_tile.wait()


def finish(tile, probe, out_tile, out_probe, tile_v, probe_v, in_sem, out_sem):
    work = []
    for piece in range(4):
        part = pl.ds(piece * PIECE, PIECE)
        for index, (src, held, dst) in enumerate(
            ((tile, tile_v, out_tile), (probe, probe_v, out_probe))
        ):
            load = pltpu.make_async_copy(src.at[:, part, :], held.at[:, part, :], in_sem.at[index, piece])
            load.start()
            work.append((load, held.at[:, part, :], dst.at[:, part, :], out_sem.at[index, piece]))
    stores = []
    for load, src, dst, sem in work:
        load.wait()
        store = pltpu.make_async_copy(src, dst, sem)
        store.start()
        stores.append(store)
    for store in stores:
        store.wait()


def on_device(rows_n, cols_n, object_field, probe, counts_measured, offsets, slot_count):
    tables, lane_tw, row_tw = constants()
    any_spec = pl.BlockSpec(memory_space=pltpu.HBM)
    smem_spec = pl.BlockSpec(memory_space=pltpu.SMEM)
    tile = (2, PS, PS)
    dma = pltpu.SemaphoreType.DMA
    shapes = (jax.ShapeDtypeStruct(tile, F32), jax.ShapeDtypeStruct(tile, F32))
    results = pl.pallas_call(
        functools.partial(kernel, rows_n, cols_n),
        out_shape=(jax.ShapeDtypeStruct(tile, F32), jax.ShapeDtypeStruct(tile, F32)),
        in_specs=[any_spec, any_spec, any_spec, smem_spec, smem_spec] + [any_spec] * 3,
        out_specs=(any_spec, any_spec),
        scratch_shapes=[
            pltpu.VMEM(tile, F32),
            pltpu.VMEM((3,) + tile, F32),
            pltpu.VMEM((CAP,) + tile, F32),
            pltpu.VMEM((CAP,) + tile, F32),
            pltpu.VMEM((1, 1, CAP, PS, PS), F32),
            pltpu.VMEM((CAP, PS, PS), F32),
            pltpu.VMEM(tile, F32),
            pltpu.VMEM((4, PS, PS), F32),
            pltpu.VMEM((4, PS, PS), BF16),
            pltpu.VMEM((2, 8, HALF), F32),
            pltpu.VMEM((2, HALF, HALF), F32),
            pltpu.VMEM((2, PS, PS), BF16),
            pltpu.VMEM((2, CAP * ROWS, PS), BF16),
            pltpu.VMEM((2, CAP * ROWS, PS), BF16),
            pltpu.VMEM((CAP, 2, PS, PS), F32),
            pltpu.VMEM((4, 2 * PS, HALF), F32),
            pltpu.VMEM((CAP, 2, 2 * PS, HALF), F32),
            pltpu.VMEM((4,) + tile, F32),
            pltpu.VMEM((4, PS, HALF), F32),
            pltpu.VMEM((2, PS, HALF), F32),
            pltpu.VMEM((3,) + tile, F32),
            pltpu.VMEM(tile, F32),
            pltpu.VMEM((4, PS, HALF), F32),
            pltpu.VMEM((4, HALF, HALF), F32),
            pltpu.VMEM((PLANE, 4, 8, HALF), F32),
            pltpu.VMEM((NEAR, 4, 8, HALF), F32),
            pltpu.VMEM((NEAR, 4, 8, HALF), F32),
            pltpu.VMEM((2, HALF, HALF), F32),
            pltpu.VMEM((PLANE, 2, 8, HALF), F32),
            pltpu.VMEM((NEAR, 2, 8, HALF), F32),
            pltpu.VMEM((NEAR, 2, 8, HALF), F32),
            dma((6,)),
            dma((3, CHUNKS)),
            dma((3, CHUNKS)),
            dma((CHUNKS,)),
            dma((4, 4)),
            dma((4, 4)),
            dma((2,)),
            dma((2,)),
            dma((2, PLANE)),
            dma((2, PLANE)),
            dma((2, NEAR)),
            dma((2, NEAR)),
            dma((2, NEAR)),
            dma((2, NEAR)),
            dma((PLANE,)),
            dma((PLANE,)),
            dma,
            dma,
            dma((9,)),
            pltpu.SemaphoreType.REGULAR((5,)),
        ],
        compiler_params=pltpu.CompilerParams(
            collective_id=0, has_side_effects=True, vmem_limit_bytes=60 << 20
        ),
        name="ptychography",
    )(
        object_field, probe, counts_measured, jnp.swapaxes(offsets, 2, 3), slot_count,
        jnp.asarray(tables), jnp.asarray(lane_tw), jnp.asarray(row_tw),
    )
    return pl.pallas_call(
        finish,
        out_shape=shapes,
        in_specs=[any_spec, any_spec],
        out_specs=(any_spec, any_spec),
        scratch_shapes=[
            pltpu.VMEM(tile, F32),
            pltpu.VMEM(tile, F32),
            dma((2, 4)),
            dma((2, 4)),
        ],
        compiler_params=pltpu.CompilerParams(vmem_limit_bytes=60 << 20),
        name="finish",
    )(*results)


def solution(mesh):
    rows_n, cols_n = mesh.shape["row"], mesh.shape["col"]
    return jax.shard_map(
        functools.partial(on_device, rows_n, cols_n),
        mesh=mesh,
        in_specs=(
            P(None, "row", "col"),
            P(),
            P("row", "col", None, None, None),
            P("row", "col", None, None),
            P("row", "col"),
        ),
        out_specs=(P(None, "row", "col"), P()),
        check_vma=False,
    )
```
